512 devices in a mesh: slab: 8 (over y, core), sub: 64 (over z, x).
Axes of the slice: x: 4, y: 4, z: 16, core: 2. Of those that a mesh axis runs over, the one named last changes fastest.
Arguments:
- source: float32 [4096, 343], P(('slab', 'sub')), may hold values from -8 to 8
- conductivity: float32 [4096], P(('slab', 'sub')), may hold values from 0.1 to 10
- basis: float32 [64, 4096, 343], P(None, ('slab', 'sub'))
- current_values: bfloat16 [131072, 343], P(('slab', 'sub')), may hold values from -6 to 6
- current_elements: int32 [131072], P(('slab', 'sub')), may hold values from 0 to 7
- current_owners: int32 [131072, 1], P(('slab', 'sub')), may hold values from 0 to 63; in each aligned block of 256 rows (0 to 255, 256 to 511, ...) at most 6 rows name the same one
- block_counts: int32 [512], P(('slab', 'sub')), may hold values from 1 to 2, as said below
Outputs:
- solution: float32 [4096, 343], P(('slab', 'sub'))
- residual: float32 [4096, 343], P(('slab', 'sub'))
The draws below stay inside these ranges and needn't reach their ends.
Inputs may be any that keep to these rules, and one draw needn't show every extreme that they name: `current_owners`: within the rows of one device at most 6 rows name any one owner, and some device's rows name one owner exactly 6 times. `block_counts`: rows in blocks at or beyond a device's count are padding and carry nothing; some device holds 2 blocks.
All inputs are finite; a program needn't handle non-finite values.
Results may differ from the reference program's by a relative error of at most 0.0006.
Values may be sent and summed in bfloat16 or wider, within the bound.
A program may use at most 128 MiB of HBM per device.

```python
import math
import jax
import jax.numpy as jnp
import numpy as np
from jax import lax

NODES = 343
NBASIS = 64
E_DEV = 8
BLOCK = 128
BLK_DEV = 2
ITERS = 3
ROWS_DEV = 256
CAP = 6
ELEMS = 4096
ROWS = 131072
N_SUB = 64
DEVICES = 512


def draw_basis(key, part):
    position = jnp.arange(ELEMS) % E_DEV
    distance = jnp.minimum(position, E_DEV - 1 - position).astype(jnp.float32)
    weight = jnp.exp(-0.5 * distance)
    values = jax.random.normal(key, (NBASIS, ELEMS, NODES), jnp.float32)
    return values * weight[None, :, None] * 0.0625


def draw_block_counts(key, part):
    counts = jax.random.randint(key, (DEVICES,), 1, BLK_DEV + 1)
    chosen = jax.random.randint(jax.random.fold_in(key, 7), (), 0, DEVICES)
    return counts.at[chosen].set(BLK_DEV)


def touch_ends(drawn, key, least, high):
    spot = [jax.random.randint(jax.random.fold_in(key, axis), (), 0, length) for axis, length in enumerate(drawn.shape)]
    main_axis = drawn.shape.index(max(drawn.shape))
    neighbour = spot[:main_axis] + [(spot[main_axis] + 1) % drawn.shape[main_axis]] + spot[main_axis + 1:]
    return drawn.at[tuple(spot)].set(least).at[tuple(neighbour)].set(high)


def shard_levels(rng, extent, split, least, largest):
    level = 1.0
    for axis_at, blocks in split:
        draws = jax.random.uniform(jax.random.fold_in(jax.random.fold_in(rng, 6), axis_at), (blocks,), jnp.float32, least / len(split), largest / len(split))
        level = level * jnp.repeat(jnp.exp(draws), extent[axis_at] // blocks).reshape((-1,) + (1,) * (len(extent) - 1 - axis_at))
    return level


def assign_block(key, own, number, rows, amount, top, limit, lean):
    order = jax.random.permutation(key, amount)
    packed, common = shares(amount, rows * top, limit, lean, True), shares(amount, rows * top, limit, lean, False)
    places = jnp.arange(amount)

    def named(tallies, rotation):
        used = int((tallies > 0).sum())
        fixed = max(1, used // 4)
        moved = fixed + (places - fixed + rotation * (used - fixed)) % max(1, amount - fixed)
        return jnp.zeros((amount,), jnp.int32).at[order[jnp.where(places < fixed, places, moved)]].set(jnp.asarray(tallies, jnp.int32))

    tallies = jnp.where(number % 4 == 0, named(packed, number // 4), named(common, number - number // 4 - 1))
    mixed = jax.random.permutation(jax.random.fold_in(own, 3), amount)
    source_of, receiver = mixed[0:amount // 2 * 2:2], mixed[1:amount // 2 * 2:2]
    margin = jnp.minimum(tallies[source_of] - 1, limit - tallies[receiver]) // 2
    margin = jnp.where((source_of == order[0]) | (receiver == order[0]) | (tallies[receiver] == 0), 0, jnp.maximum(margin, 0))
    moved = jax.random.randint(jax.random.fold_in(own, 4), (amount // 2,), 0, 1 << 20) % (margin + 1)
    tallies = tallies.at[source_of].add(-moved).at[receiver].add(moved)
    labels = jnp.searchsorted(jnp.cumsum(tallies), jnp.arange(rows * top), side="right").astype(jnp.int32)
    table = labels.reshape(top, rows).T
    table = table[jax.random.permutation(jax.random.fold_in(own, 1), rows)]
    rotation = jax.random.randint(jax.random.fold_in(own, 2), (rows, 1), 0, top)
    return jnp.take_along_axis(table, (jnp.arange(top)[None, :] + rotation) % top, axis=1)


def shares(amount, total, limit, skew, full):
    loads = [(1 << 20) // math.isqrt(grade ** skew) + 1 for grade in range(1, amount + 1)]
    largest = limit if full else min(limit, max(-(-total // amount), total * loads[0] // sum(loads)))
    least = 1 if total - largest >= amount - 1 else 0
    given, surplus = [largest] + [least] * (amount - 1), total - largest - least * (amount - 1)
    while surplus > 0:
        candidates = [i for i in range(1, amount) if given[i] < largest] or [i for i in range(1, amount) if given[i] < limit]
        pool, left = sum([loads[i] for i in candidates]), surplus
        for i in candidates:
            more = min(limit - given[i], max(1, left * loads[i] // pool), surplus)
            given[i] = given[i] + more
            surplus = surplus - more
    return np.array(given)


def centred(own_key, extent, scale, reach, shards=(), kind=jnp.bfloat16):
    entries = jax.random.normal(own_key, extent, jnp.float32) * scale
    if len(shards) > 0:
        entries = shard_levels(own_key, extent, shards, -0.22, 0.18) * entries
    return jnp.clip(entries, min=-reach, max=reach).astype(kind)


def setup_inputs(seed: int = 0) -> dict:
    streams_of = jax.random.split(jax.random.key(seed), 8)
    source = centred(streams_of[0], (ELEMS, NODES), 1.0, 8.0, ((0, 512),), jnp.float32)
    conductivity = jnp.clip(jnp.exp(math.log(10.0) - 4.6051702 * jax.random.uniform(streams_of[1], (ELEMS,), jnp.float32) ** shard_levels(streams_of[1], (ELEMS,), ((0, 512),), -0.2, 0.2)), 0.1, 10.0)
    basis = draw_basis(jax.random.fold_in(streams_of[7], 71), 0)
    current_values = centred(streams_of[3], (ROWS, NODES), 1.0, 6.0, ((0, 512),))
    current_elements = touch_ends(jax.random.randint(streams_of[4], (ROWS,), 0, E_DEV), jax.random.fold_in(streams_of[4], 1), 0, E_DEV - 1).astype(jnp.int32)
    current_owners_keys = jax.random.split(jax.random.fold_in(streams_of[5], 1), ROWS // ROWS_DEV)
    current_owners_turns = jax.random.permutation(jax.random.fold_in(streams_of[5], 3), ROWS // ROWS_DEV)
    current_owners = jax.vmap(lambda own, number: assign_block(jax.random.fold_in(streams_of[5], 2), own, number, ROWS_DEV, N_SUB, 1, CAP, 2))(current_owners_keys, current_owners_turns).reshape((ROWS, 1))
    block_counts = draw_block_counts(jax.random.fold_in(streams_of[7], 71), 0)
    return {"source": source, "conductivity": conductivity, "basis": basis, "current_values": current_values, "current_elements": current_elements, "current_owners": current_owners, "block_counts": block_counts}


penalty = 10.0
relaxation = 0.2
highest = lax.Precision.HIGHEST

def element_matrix():
    points = jnp.arange(7)
    at_ends = ((points == 0) | (points == 6)).astype(jnp.float32)
    second = jnp.diag(2.0 - at_ends) - (jnp.abs(points[:, None] - points[None, :]) == 1).astype(jnp.float32)
    identity = jnp.eye(7, dtype=jnp.float32)
    return jnp.kron(jnp.kron(second, identity), identity) + jnp.kron(jnp.kron(identity, second), identity) + jnp.kron(identity, jnp.kron(identity, second))

def face_mask():
    node_ids = jnp.arange(343)
    return ((node_ids < 49) | (node_ids >= 294)).astype(jnp.float32)

def couple(field, conductivity, stiffness, prev_right, next_left):
    left_term = penalty * (field[..., :49] - prev_right)
    right_term = penalty * (field[..., 294:] - next_left)
    middle = jnp.zeros(field.shape[:-1] + (245,), jnp.float32)
    return conductivity[:, None] * stiffness + relaxation * field + jnp.concatenate([left_term, middle, right_term], axis=-1)

def apply_chain(field, conductivity, kel):
    stiffness = jnp.dot(field.astype(jnp.float32), kel.astype(jnp.float32), precision=highest, preferred_element_type=jnp.float32)
    prev_right = jnp.pad(field[:-1, 294:], ((1, 0), (0, 0)))
    next_left = jnp.pad(field[1:, :49], ((0, 1), (0, 0)))
    return couple(field, conductivity, stiffness, prev_right, next_left)

def apply_block(sub_basis, conductivity, kel):
    stiffness = jnp.dot(sub_basis.reshape(-1, 343).astype(jnp.float32), kel.astype(jnp.float32), precision=highest, preferred_element_type=jnp.float32).reshape(sub_basis.shape)
    prev_right = jnp.pad(sub_basis[:, :-1, 294:], ((0, 0), (1, 0), (0, 0)))
    next_left = jnp.pad(sub_basis[:, 1:, :49], ((0, 0), (0, 1), (0, 0)))
    return couple(sub_basis, conductivity, stiffness, prev_right, next_left)

def invert(matrix):
    factor = jnp.linalg.cholesky(matrix)
    identity = jnp.eye(matrix.shape[0], dtype=jnp.float32)
    solved = lax.linalg.triangular_solve(factor, identity, left_side=True, lower=True)
    return jnp.dot(solved.T.astype(jnp.float32), solved.astype(jnp.float32), precision=highest, preferred_element_type=jnp.float32)

def reference(source, conductivity, basis, current_values, current_elements, current_owners, block_counts):
    kel = element_matrix()
    diagonal = conductivity[:, None] * jnp.diagonal(kel)[None, :] + relaxation + penalty * face_mask()[None, :]
    row_ids = jnp.arange(ROWS_DEV * DEVICES, dtype=jnp.int32)
    device = row_ids // ROWS_DEV
    is_live = row_ids % ROWS_DEV // BLOCK < block_counts[device]
    target = device // N_SUB * (N_SUB * E_DEV) + current_owners[:, 0] * E_DEV + current_elements
    target = jnp.where(is_live, target, ELEMS)
    currents = jnp.zeros((ELEMS, 343), jnp.float32).at[target].add(current_values.astype(jnp.float32), mode='drop')
    rhs = source + currents

    def coarse_block(index):
        sub_basis = lax.dynamic_slice_in_dim(basis, index * E_DEV, E_DEV, 1)
        local_sigma = lax.dynamic_slice_in_dim(conductivity, index * E_DEV, E_DEV, 0)
        applied = apply_block(sub_basis, local_sigma, kel)
        matrix = jnp.einsum('kep,lep->kl', sub_basis, applied, precision=highest)
        return invert(matrix)
    inverses = lax.map(coarse_block, jnp.arange(DEVICES, dtype=jnp.int32))
    width = basis.shape[0]
    last_right = basis[:, E_DEV - 1::E_DEV, 294:]
    first_left = basis[:, ::E_DEV, :49]
    zero_block = jnp.zeros((1, width, width), jnp.float32)
    right_inner = -penalty * jnp.einsum('ksn,lsn->skl', last_right[:, :-1], first_left[:, 1:], precision=highest)
    left_inner = -penalty * jnp.einsum('ksn,lsn->skl', first_left[:, 1:], last_right[:, :-1], precision=highest)
    right_blocks = jnp.concatenate([right_inner, zero_block], axis=0)
    left_blocks = jnp.concatenate([zero_block, left_inner], axis=0)
    shaped = basis.reshape(width, DEVICES, E_DEV, 343)

    def precondition(residual):
        pieces = residual.reshape(DEVICES, E_DEV, 343)
        projected = jnp.einsum('ksep,sep->sk', shaped, pieces, precision=highest)
        first_pass = jnp.einsum('skl,sl->sk', inverses, projected, precision=highest)
        before = jnp.pad(first_pass[:-1], ((1, 0), (0, 0)))
        following = jnp.pad(first_pass[1:], ((0, 1), (0, 0)))
        corrected = projected - jnp.einsum('skl,sl->sk', left_blocks, before, precision=highest) - jnp.einsum('skl,sl->sk', right_blocks, following, precision=highest)
        second_pass = jnp.einsum('skl,sl->sk', inverses, corrected, precision=highest)
        coarse = jnp.einsum('ksep,sk->sep', shaped, second_pass, precision=highest).reshape(ELEMS, 343)
        return residual / diagonal + coarse
    solution = jnp.zeros_like(rhs)
    residual = rhs
    precond = precondition(residual)
    direction = precond
    inner_now = jnp.sum(residual * precond)
    for iteration in range(ITERS):
        applied = apply_chain(direction, conductivity, kel)
        step_size = inner_now / jnp.sum(direction * applied)
        solution = solution + step_size * direction
        residual = residual - step_size * applied
        if iteration + 1 < ITERS:
            precond = precondition(residual)
            inner_next = jnp.sum(residual * precond)
            direction = precond + inner_next / inner_now * direction
            inner_now = inner_next
    return (solution, residual)
```

```python
import functools

import jax
import jax.numpy as jnp
import numpy as np
from jax import lax
from jax.experimental import pallas as pl
from jax.experimental.pallas import tpu as pltpu
from jax.sharding import PartitionSpec as P

BLOCK = 128
CAP = 6
NODES = 343
WIDE = 384
FACE = 49
EL = 8
NB = 64
XN = 4
MARK = 120
SHIFT = 1.0
PENALTY = 10.0
RELAX = 0.2
HIGH = lax.Precision.HIGHEST
F32 = jnp.float32
BF16 = jnp.bfloat16
NT = (((1,), (1,)), ((), ()))
TN = (((0,), (0,)), ((), ()))


def stencil_constants():
    second = np.diag(np.array([1.0, 2, 2, 2, 2, 2, 1]))
    for i in range(6):
        second[i, i + 1] = second[i + 1, i] = -1.0
    one = np.eye(7)
    kel = (
        np.kron(np.kron(second, one), one)
        + np.kron(np.kron(one, second), one)
        + np.kron(one, np.kron(one, second))
    )
    full = np.zeros((WIDE, WIDE), np.float32)
    full[:NODES, :NODES] = kel
    return full, np.diagonal(full)


def split2(value):
    hi = value.astype(BF16)
    lo = (value - hi.astype(F32)).astype(BF16)
    return hi, lo


def iota(shape, dim):
    return lax.broadcasted_iota(jnp.int32, shape, dim)


def dot(a, b, dims=(((1,), (0,)), ((), ())), precision=None):
    return lax.dot_general(a, b, dims, precision=precision, preferred_element_type=F32)


def kernel(
    slabs,
    subs,
    cond_ref,
    count_ref,
    src_ref,
    basis_ref,
    vals_ref,
    elem_ref,
    own_ref,
    kel_ref,
    kdiag_ref,
    x_out,
    r_out,
    vext,
    a_src,
    a_dst,
    b_src,
    b_dst,
    bt_ref,
    cz_ref,
    padded,
    source_ref,
    g_src,
    g_dst,
    f_src,
    f_dst,
    s_src,
    s_dst,
    a_sem,
    b_sem,
    g_sem,
    f_sem,
    s_sem,
):
    zn = subs // XN
    total = slabs * subs
    slab = lax.axis_index("slab")
    sub = lax.axis_index("sub")
    x = lax.rem(sub, XN)
    z = lax.div(sub, XN)
    chain = slab * subs + sub
    rows = vals_ref.shape[0]
    slot = zn * CAP

    def x_peer(i):
        return (slab, z * XN + lax.rem(x + i, XN))

    def z_peer(i):
        return (slab, lax.rem(z + i, zn) * XN + x)

    def slab_peer(i):
        return (lax.rem(slab + i, slabs), sub)

    def chain_peer(step):
        other = lax.rem(chain + step + total, total)
        return (lax.div(other, subs), lax.rem(other, subs))

    peers = (
        [x_peer(i) for i in range(1, XN)]
        + [z_peer(i) for i in range(1, zn)]
        + [slab_peer(i) for i in range(1, slabs)]
        + [chain_peer(step) for step in (-1, 1, -2, 2)]
    )
    barrier = pltpu.get_barrier_semaphore()
    for peer in peers:
        pl.semaphore_signal(
            barrier, inc=1, device_id=peer, device_id_type=pl.DeviceIdType.MESH
        )

    def send(src, dst, sems, k, peer):
        copy = pltpu.make_async_remote_copy(
            src_ref=src,
            dst_ref=dst,
            send_sem=sems.at[0, k],
            recv_sem=sems.at[1, k],
            device_id=peer,
            device_id_type=pl.DeviceIdType.MESH,
        )
        copy.start()
        return copy

    order = iota((subs, rows), 0)
    order = lax.rem(order, zn) * XN + lax.div(order, zn)
    live = lax.div(iota((subs, rows), 1), BLOCK) < count_ref[0]
    owned = ((own_ref[...] == order) & live).astype(F32)
    before = (iota((rows, rows), 0) < iota((rows, rows), 1)).astype(BF16)
    rank = dot(owned.astype(BF16), before)
    pieces = []
    for to in range(XN):
        mine = owned[to * zn : (to + 1) * zn]
        place = rank[to * zn : (to + 1) * zn]
        for j in range(CAP):
            pieces.append(jnp.where(place == float(j), mine, 0.0))
    select = jnp.concatenate(pieces, axis=0).astype(BF16)
    vext[:, 256:] = jnp.zeros((rows, 128), BF16)
    vext[:, :NODES] = vals_ref[...]
    marks = (elem_ref[...] == iota((128, rows), 0) - MARK).astype(BF16)
    moved = dot(select, vext[...])
    marked = dot(select, marks, NT)
    a_src[:, :, :256] = moved[:, :256].astype(BF16).reshape(XN, slot, 256)
    a_src[:, :, 256:] = (moved[:, 256:] + marked).astype(BF16).reshape(XN, slot, 128)

    pl.semaphore_wait(barrier, len(peers))
    a_copies = [
        send(a_src.at[lax.rem(x + i, XN)], a_dst.at[i], a_sem, i, x_peer(i))
        for i in range(1, XN)
    ]
    a_dst[0] = a_src[x]

    lane = iota((1, WIDE), 1)
    left = lane < FACE
    right = (lane >= NODES - FACE) & (lane < NODES)
    facew = jnp.where(left | right, PENALTY, 0.0)
    flat = basis_ref[...].reshape(NB * EL, NODES)
    padded[2] = jnp.zeros((NB * EL, 128), F32)
    padded[0] = flat[:, 0:128]
    padded[1] = flat[:, 128:256]
    padded[2, :, : NODES - 256] = flat[:, 256:]
    for t in range(3):
        for e in range(EL):
            at = e * WIDE + t * 128
            bt_ref[:, at : at + 128] = padded[t, pl.ds(e, NB, stride=EL), :]

    def element(ref, e):
        return ref[:, e * WIDE : (e + 1) * WIDE]

    kel = kel_ref[...]
    applied = []
    for e in range(EL):
        be = element(bt_ref, e)
        hi, lo = split2(be)
        stiff = dot(hi, kel) + dot(lo, kel)
        out = cond_ref[e] * stiff + (RELAX + facew) * be
        if e > 0:
            turned = pltpu.roll(element(bt_ref, e - 1), WIDE - NODES + FACE, 1)
            out = out - jnp.where(left, PENALTY * turned, 0.0)
        if e < EL - 1:
            turned = pltpu.roll(element(bt_ref, e + 1), NODES - FACE, 1)
            out = out - jnp.where(right, PENALTY * turned, 0.0)
        applied.append(out)
    matrix = dot(bt_ref[...], jnp.concatenate(applied, axis=1), NT, HIGH)

    for copy in a_copies:
        copy.wait()
    arrived = a_dst[...].reshape(XN * slot, WIDE)
    spread = (iota((128, 128), 0) == MARK + lax.rem(iota((128, 128), 1), EL)).astype(BF16)
    spread = dot(arrived[:, 256:], spread)
    keep = lax.rem(iota(spread.shape, 0), zn) == lax.div(iota(spread.shape, 1), EL)
    weights = jnp.where(keep, spread, 0.0)
    sums = dot(weights.T.astype(BF16), arrived)
    b_src[...] = sums[: zn * EL].reshape(zn, EL, WIDE)
    b_copies = [
        send(b_src.at[lax.rem(z + i, zn)], b_dst.at[i], b_sem, i, z_peer(i))
        for i in range(1, zn)
    ]
    b_dst[0] = b_src[z]

    unit = (iota((NB, NB), 0) == iota((NB, NB), 1)).astype(F32)
    work = jnp.concatenate([matrix, unit], axis=1)
    row_id = iota((NB, 2 * NB), 0)
    for k in range(NB):
        row = work[k : k + 1, :] / work[k : k + 1, k : k + 1]
        work = jnp.where(row_id == k, row, work - work[:, k : k + 1] * row)
    inverse = work[:, NB:]
    cz_ref[...] = dot(inverse, bt_ref[...], precision=HIGH)

    low = iota((1, 128), 1)
    near = low < FACE

    def left_face(value):
        return jnp.where(near, value[:, 0:128], 0.0)

    def right_face(value):
        return jnp.where(near, pltpu.roll(value[:, 256:WIDE], 128 - 38, 1), 0.0)

    w = PENALTY * (
        left_face(element(cz_ref, 0))
        + pltpu.roll(right_face(element(cz_ref, EL - 1)), 64, 1)
    )
    face_l = left_face(element(bt_ref, 0))
    face_r = right_face(element(bt_ref, EL - 1))
    g_src[0] = dot(face_l.T, w, precision=HIGH)[:56]
    g_src[1] = dot(face_r.T, w, precision=HIGH)[:56]
    g_copies = [
        send(g_src.at[0], g_dst.at[0], g_sem, 0, chain_peer(-1)),
        send(g_src.at[1], g_dst.at[1], g_sem, 1, chain_peer(1)),
    ]

    el_row = iota((EL, WIDE), 0)
    conduct = jnp.zeros((EL, WIDE), F32)
    for e in range(EL):
        conduct = jnp.where(el_row == e, cond_ref[e], conduct)
    diagonal = conduct * kdiag_ref[...] + RELAX + facew
    inner_lane = iota((EL, WIDE), 1) < NODES
    source_ref[:, 256:] = jnp.zeros((EL, 128), F32)
    source_ref[:, :NODES] = src_ref[...]
    for copy in b_copies:
        copy.wait()
    currents = b_dst[0]
    for i in range(1, zn):
        currents = currents + b_dst[i]
    rhs = source_ref[...] + jnp.where(inner_lane, currents, 0.0)

    has = {step: (chain + step >= 0) & (chain + step < total) for step in (-2, -1, 1, 2)}
    eye = iota((56, 128), 0) == iota((56, 128), 1)

    def turn(matrix, vector):
        column = jnp.sum(matrix * vector, axis=1, keepdims=True)
        return jnp.sum(jnp.where(eye, column, 0.0), axis=0, keepdims=True)

    def lift(column):
        line = jnp.sum(bt_ref[...] * column, axis=0, keepdims=True)
        return jnp.concatenate(
            [line[:, e * WIDE : (e + 1) * WIDE] for e in range(EL)], axis=0
        )

    def gram(a, b):
        prod = a * b
        prod = prod[:, 0:128] + prod[:, 128:256] + prod[:, 256:384]
        return jnp.sum(prod, axis=0, keepdims=True)

    pad_row = jnp.zeros((1, 256), F32)
    residuals, preconds = [rhs], []
    products = {}
    all_copies = []
    for k in range(3):
        res = residuals[k]
        scaled = res / diagonal
        acc = jnp.zeros((NB, WIDE), F32)
        for e in range(EL):
            acc = acc + element(cz_ref, e) * res[e : e + 1, :]
        acc = acc[:, 0:128] + acc[:, 128:256] + acc[:, 256:384]
        first = lift(jnp.sum(acc, axis=1, keepdims=True))
        fl = left_face(first[0:1])
        fr = right_face(first[EL - 1 : EL])
        el = left_face(scaled[0:1]) + fl
        er = right_face(scaled[EL - 1 : EL]) + fr
        f_src[k] = jnp.concatenate([fl, fr, el, er, jnp.zeros((4, 128), F32)], axis=0)
        copies = [
            send(f_src.at[k], f_dst.at[k, i], f_sem, 4 * k + i, chain_peer(step))
            for i, step in enumerate((-1, 1, -2, 2))
        ]
        for i in range(k + 1):
            for j in range(k):
                if (i, j) not in products:
                    products[i, j] = gram(residuals[i], preconds[j])
        partial = scaled + first
        if k == 0:
            for copy in g_copies:
                copy.wait()
        for copy in copies:
            copy.wait()
        after1 = jnp.where(has[1], f_dst[k, 0], 0.0)
        before1 = jnp.where(has[-1], f_dst[k, 1], 0.0)
        after2 = jnp.where(has[2], f_dst[k, 2], 0.0)
        before2 = jnp.where(has[-2], f_dst[k, 3], 0.0)
        own_v = before1[1:2] + pltpu.roll(after1[0:1], 64, 1)
        after_v = fr + pltpu.roll(after2[0:1], 64, 1)
        before_v = before2[1:2] + pltpu.roll(fl, 64, 1)
        pre = partial + lift(jnp.sum(w * own_v, axis=1, keepdims=True))
        after_face = jnp.where(has[1], after1[2:3] + turn(g_dst[0], after_v), 0.0)
        before_face = jnp.where(has[-1], before1[3:4] + turn(g_dst[1], before_v), 0.0)
        hi, lo = split2(pre)
        both = jnp.concatenate([hi.astype(F32), lo.astype(F32)], axis=0).astype(BF16)
        stiff = dot(both, kel)
        stiff = stiff[0:EL] + stiff[EL : 2 * EL]
        from_left = pltpu.roll(pltpu.roll(pre, 1, 0), WIDE - NODES + FACE, 1)
        from_left = jnp.where(
            el_row == 0, jnp.concatenate([before_face, pad_row], axis=1), from_left
        )
        from_right = pltpu.roll(pltpu.roll(pre, EL - 1, 0), NODES - FACE, 1)
        from_right = jnp.where(
            el_row == EL - 1,
            jnp.concatenate([pad_row, pltpu.roll(after_face, 38, 1)], axis=1),
            from_right,
        )
        image = conduct * stiff + (RELAX + facew) * pre
        image = image - PENALTY * (
            jnp.where(left, from_left, 0.0) + jnp.where(right, from_right, 0.0)
        )
        preconds.append(pre)
        residuals.append(image - SHIFT * res)

    for i in range(4):
        for j in range(3):
            if (i, j) not in products:
                products[i, j] = gram(residuals[i], preconds[j])
    share = jnp.concatenate(
        [products[i, j] for i in range(4) for j in range(3)] + [jnp.zeros((4, 128), F32)], axis=0
    )
    at = 0
    for stage, (count, peer) in enumerate(((XN, x_peer), (zn, z_peer), (slabs, slab_peer))):
        s_src[stage] = share
        copies = [
            send(s_src.at[stage], s_dst.at[at + i - 1], s_sem, at + i - 1, peer(i))
            for i in range(1, count)
        ]
        for copy in copies:
            copy.wait()
        for i in range(1, count):
            share = share + s_dst[at + i - 1]
        at += count - 1

    sums = jnp.sum(share, axis=1, keepdims=True)
    n = [[sums[3 * i + j : 3 * i + j + 1] for j in range(3)] for i in range(4)]

    def form(p, q):
        value = 0.0
        for i, a in enumerate(p):
            line = 0.0
            for j, b in enumerate(q):
                line = line + n[i][j] * b
            value = value + a * line
        return value

    zero = jnp.zeros((1, 1), F32)
    one = jnp.ones((1, 1), F32)
    res_c = [one]
    dir_c = [one]
    sol_c = [zero, zero, zero]
    inner = form(res_c, res_c)
    for k in range(3):
        image_c = [zero] + dir_c
        image_c = [v + SHIFT * u for v, u in zip(image_c, dir_c + [zero])]
        step = inner / form(image_c, dir_c)
        for j, v in enumerate(dir_c):
            sol_c[j] = sol_c[j] + step * v
        res_c = [u - step * v for u, v in zip(res_c + [zero], image_c)]
        if k < 2:
            fresh = form(res_c, res_c)
            ratio = fresh / inner
            dir_c = [u + ratio * v for u, v in zip(res_c, dir_c + [zero])]
            inner = fresh
    answer = sum(sol_c[j] * preconds[j] for j in range(3))
    remain = sum(res_c[j] * residuals[j] for j in range(4))
    x_out[...] = answer[:, :NODES]
    r_out[...] = remain[:, :NODES]


def on_device(slabs, subs, source, conductivity, basis, values, elements, owners, counts):
    rows = values.shape[0]
    zn = subs // XN
    kel, kdiag = stencil_constants()
    vmem = pl.BlockSpec(memory_space=pltpu.VMEM)
    smem = pl.BlockSpec(memory_space=pltpu.SMEM)
    slot = zn * CAP
    peers = XN + zn + slabs - 3
    dma = pltpu.SemaphoreType.DMA
    out = jax.ShapeDtypeStruct(source.shape, F32)
    return pl.pallas_call(
        functools.partial(kernel, slabs, subs),
        out_shape=(out, out),
        in_specs=[smem, smem] + [vmem] * 7,
        out_specs=(vmem, vmem),
        scratch_shapes=[
            pltpu.VMEM((rows, WIDE), BF16),
            pltpu.VMEM((XN, slot, WIDE), BF16),
            pltpu.VMEM((XN, slot, WIDE), BF16),
            pltpu.VMEM((zn, EL, WIDE), F32),
            pltpu.VMEM((zn, EL, WIDE), F32),
            pltpu.VMEM((NB, EL * WIDE), F32),
            pltpu.VMEM((NB, EL * WIDE), F32),
            pltpu.VMEM((3, NB * EL, 128), F32),
            pltpu.VMEM((EL, WIDE), F32),
            pltpu.VMEM((2, 56, 128), F32),
            pltpu.VMEM((2, 56, 128), F32),
            pltpu.VMEM((3, 8, 128), F32),
            pltpu.VMEM((3, 4, 8, 128), F32),
            pltpu.VMEM((3, 16, 128), F32),
            pltpu.VMEM((peers, 16, 128), F32),
            dma((2, XN)),
            dma((2, zn)),
            dma((2, 2)),
            dma((2, 12)),
            dma((2, peers)),
        ],
        compiler_params=pltpu.CompilerParams(
            collective_id=0, has_side_effects=True, vmem_limit_bytes=48 * 1024 * 1024
        ),
    )(
        conductivity,
        counts,
        source,
        basis,
        values,
        elements.reshape(1, rows),
        owners.reshape(1, rows),
        jnp.asarray(kel, BF16),
        jnp.asarray(kdiag.reshape(1, WIDE)),
    )


def solution(mesh):
    both = ("slab", "sub")
    placed = (
        P(both, None),
        P(both),
        P(None, both, None),
        P(both, None),
        P(both),
        P(both, None),
        P(both),
    )
    return jax.shard_map(
        functools.partial(on_device, mesh.shape["slab"], mesh.shape["sub"]),
        mesh=mesh,
        in_specs=placed,
        out_specs=(P(both, None), P(both, None)),
        check_vma=False,
    )
```

```python
import functools

import jax
import jax.numpy as jnp
import numpy as np
from jax import lax
from jax.experimental import pallas as pl
from jax.experimental.pallas import tpu as pltpu
from jax.sharding import PartitionSpec as P

BLOCK = 128
CAP = 6
NODES = 343
WIDE = 384
FACE = 49
EL = 8
NB = 64
XN = 4
MARK = 120
SHIFT = 1.0
PENALTY = 10.0
RELAX = 0.2
HIGH = lax.Precision.HIGHEST
F32 = jnp.float32
BF16 = jnp.bfloat16
NT = (((1,), (1,)), ((), ()))
TN = (((0,), (0,)), ((), ()))


def stencil_constants():
    second = np.diag(np.array([1.0, 2, 2, 2, 2, 2, 1]))
    for i in range(6):
        second[i, i + 1] = second[i + 1, i] = -1.0
    one = np.eye(7)
    kel = (
        np.kron(np.kron(second, one), one)
        + np.kron(np.kron(one, second), one)
        + np.kron(one, np.kron(one, second))
    )
    full = np.zeros((WIDE, WIDE), np.float32)
    full[:NODES, :NODES] = kel
    full[NODES + 1] = np.diagonal(full)
    return full


def split2(value):
    hi = value.astype(BF16)
    lo = (value - hi.astype(F32)).astype(BF16)
    return hi, lo


def iota(shape, dim):
    return lax.broadcasted_iota(jnp.int32, shape, dim)


def dot(a, b, dims=(((1,), (0,)), ((), ())), precision=None):
    return lax.dot_general(a, b, dims, precision=precision, preferred_element_type=F32)


def kernel(
    slabs,
    subs,
    cond_ref,
    count_ref,
    src_ref,
    basis_ref,
    vals_ref,
    elem_ref,
    own_ref,
    kel_ref,
    x_out,
    r_out,
    cond_in,
    count_in,
    src_in,
    basis_in,
    vals_in,
    elem_in,
    own_in,
    kel_in,
    a_src,
    a_dst,
    b_src,
    b_dst,
    bt_ref,
    cz_ref,
    padded,
    source_ref,
    g_src,
    g_dst,
    f_src,
    f_dst,
    s_src,
    s_dst,
    a_sem,
    b_sem,
    g_sem,
    f_sem,
    s_sem,
    in_sem,
):
    zn = subs // XN
    total = slabs * subs
    slab = lax.axis_index("slab")
    sub = lax.axis_index("sub")
    x = lax.rem(sub, XN)
    z = lax.div(sub, XN)
    chain = slab * subs + sub
    rows = vals_ref.shape[1]
    slot = zn * CAP

    def x_peer(i):
        return (slab, z * XN + lax.rem(x + i, XN))

    def z_peer(i):
        return (slab, lax.rem(z + i, zn) * XN + x)

    def plane_peer(i, j):
        return (lax.rem(slab + 2 * j, slabs), z * XN + lax.rem(x + i, XN))

    core_peer = (slab + 1 - 2 * lax.rem(slab, 2), sub)
    ys = slabs // 2
    far = sorted(range(1, zn), key=lambda i: -min(i, zn - i))
    plane = [(i, j) for i in range(XN) for j in range(ys) if i or j]
    plane.sort(key=lambda p: -min(p[0], XN - p[0]) - min(p[1], ys - p[1]))
    x_order = sorted(range(1, XN), key=lambda i: -min(i, XN - i))

    def chain_peer(step):
        other = lax.rem(chain + step + total, total)
        return (lax.div(other, subs), lax.rem(other, subs))

    peers = (
        [z_peer(i) for i in far]
        + [chain_peer(step) for step in (-2, 2, -1, 1)]
        + [plane_peer(i, j) for i, j in plane]
        + [core_peer]
    )
    barrier = pltpu.get_barrier_semaphore()
    for peer in peers:
        pl.semaphore_signal(
            barrier, inc=1, device_id=peer, device_id_type=pl.DeviceIdType.MESH
        )

    def send(src, dst, sems, k, peer):
        copy = pltpu.make_async_remote_copy(
            src_ref=src,
            dst_ref=dst,
            send_sem=sems.at[0, k],
            recv_sem=sems.at[1, k],
            device_id=peer,
            device_id_type=pl.DeviceIdType.MESH,
        )
        copy.start()
        return copy

    fetches = [
        pltpu.make_async_copy(src, dst, in_sem.at[k])
        for k, (src, dst) in enumerate(
            (
                (own_ref, own_in),
                (count_ref, count_in),
                (elem_ref, elem_in),
                (vals_ref, vals_in),
                (basis_ref, basis_in),
                (kel_ref, kel_in),
                (cond_ref, cond_in),
                (src_ref, src_in),
            )
        )
    ]
    for fetch in fetches:
        fetch.start()

    for fetch in fetches[:4]:
        fetch.wait()
    order = iota((subs, rows), 0)
    order = lax.rem(order, zn) * XN + lax.div(order, zn)
    live = lax.div(iota((subs, rows), 1), BLOCK) < count_in[0]
    owned = ((own_in[...] == order) & live).astype(F32)
    before = (iota((rows, rows), 0) < iota((rows, rows), 1)).astype(BF16)
    rank = dot(owned.astype(BF16), before)
    pieces = []
    for to in range(XN):
        mine = owned[to * zn : (to + 1) * zn]
        place = rank[to * zn : (to + 1) * zn]
        for j in range(CAP):
            pieces.append(jnp.where(place == float(j), mine, 0.0))
    select = jnp.concatenate(pieces, axis=0).astype(BF16)
    marks = (elem_in[...] == iota((128, rows), 0) - MARK).astype(BF16)
    moved = dot(select, vals_in[...], NT).astype(BF16)
    marked = dot(select, marks, NT).astype(BF16)
    a_src[:, :, :256] = moved[:, :256].reshape(XN, slot, 256)
    a_src[:, :, 256:] = marked.reshape(XN, slot, 128)
    a_src[:, :, 256:NODES] = moved[:, 256:].reshape(XN, slot, NODES - 256)

    pl.semaphore_wait(barrier, len(peers))
    a_copies = [
        send(a_src.at[lax.rem(x + i, XN)], a_dst.at[i], a_sem, i, x_peer(i))
        for i in x_order
    ]
    a_dst[0] = a_src[x]

    for fetch in fetches[4:]:
        fetch.wait()
    lane = iota((1, WIDE), 1)
    left = lane < FACE
    right = (lane >= NODES - FACE) & (lane < NODES)
    facew = jnp.where(left | right, PENALTY, 0.0)
    flat = basis_in[...].reshape(NB * EL, NODES)
    padded[2] = jnp.zeros((NB * EL, 128), F32)
    padded[0] = flat[:, 0:128]
    padded[1] = flat[:, 128:256]
    padded[2, :, : NODES - 256] = flat[:, 256:]
    for t in range(3):
        for e in range(EL):
            at = e * WIDE + t * 128
            bt_ref[:, at : at + 128] = padded[t, pl.ds(e, NB, stride=EL), :]

    def element(ref, e):
        return ref[:, e * WIDE : (e + 1) * WIDE]

    kel = kel_in[...]
    applied = []
    for e in range(EL):
        be = element(bt_ref, e)
        hi, lo = split2(be)
        stiff = dot(hi, kel) + dot(lo, kel)
        out = cond_in[e] * stiff + (RELAX + facew) * be
        if e > 0:
            turned = pltpu.roll(element(bt_ref, e - 1), WIDE - NODES + FACE, 1)
            out = out - jnp.where(left, PENALTY * turned, 0.0)
        if e < EL - 1:
            turned = pltpu.roll(element(bt_ref, e + 1), NODES - FACE, 1)
            out = out - jnp.where(right, PENALTY * turned, 0.0)
        applied.append(out)
    matrix = dot(bt_ref[...], jnp.concatenate(applied, axis=1), NT, HIGH)

    for copy in a_copies:
        copy.wait()
    arrived = a_dst[...].reshape(XN * slot, WIDE)
    spread = (iota((128, 128), 0) == MARK + lax.rem(iota((128, 128), 1), EL)).astype(BF16)
    spread = dot(arrived[:, 256:], spread)
    keep = lax.rem(iota(spread.shape, 0), zn) == lax.div(iota(spread.shape, 1), EL)
    weights = jnp.where(keep, spread, 0.0)
    sums = dot(weights.T.astype(BF16), arrived)
    b_src[...] = sums[: zn * EL].reshape(zn, EL, WIDE)
    b_copies = [
        send(b_src.at[lax.rem(z + i, zn)], b_dst.at[i], b_sem, i, z_peer(i))
        for i in far
    ]
    b_dst[0] = b_src[z]

    unit = (iota((NB, NB), 0) == iota((NB, NB), 1)).astype(F32)
    work = jnp.concatenate([matrix, unit], axis=1)
    row_id = iota((NB, 2 * NB), 0)
    for k in range(NB):
        row = work[k : k + 1, :] / work[k : k + 1, k : k + 1]
        work = jnp.where(row_id == k, row, work - work[:, k : k + 1] * row)
    inverse = work[:, NB:]
    cz_ref[...] = dot(inverse, bt_ref[...], precision=HIGH)

    low = iota((1, 128), 1)
    near = low < FACE

    def left_face(value):
        return jnp.where(near, value[:, 0:128], 0.0)

    def right_face(value):
        return jnp.where(near, pltpu.roll(value[:, 256:WIDE], 128 - 38, 1), 0.0)

    w = PENALTY * (
        left_face(element(cz_ref, 0))
        + pltpu.roll(right_face(element(cz_ref, EL - 1)), 64, 1)
    )
    face_l = left_face(element(bt_ref, 0))
    face_r = right_face(element(bt_ref, EL - 1))
    g_src[0] = dot(face_l.T, w, precision=HIGH)[:56]
    g_src[1] = dot(face_r.T, w, precision=HIGH)[:56]
    g_copies = [
        send(g_src.at[0], g_dst.at[0], g_sem, 0, chain_peer(-1)),
        send(g_src.at[1], g_dst.at[1], g_sem, 1, chain_peer(1)),
    ]

    el_row = iota((EL, WIDE), 0)
    conduct = jnp.zeros((EL, WIDE), F32)
    for e in range(EL):
        conduct = jnp.where(el_row == e, cond_in[e], conduct)
    kdiag = kel_in[NODES - 7 : NODES + 9].astype(F32)[8:9]
    diagonal = conduct * kdiag + RELAX + facew
    inner_lane = iota((EL, WIDE), 1) < NODES
    source_ref[:, 256:] = jnp.zeros((EL, 128), F32)
    source_ref[:, :NODES] = src_in[...]
    for copy in b_copies:
        copy.wait()
    currents = b_dst[0]
    for i in range(1, zn):
        currents = currents + b_dst[i]
    rhs = source_ref[...] + jnp.where(inner_lane, currents, 0.0)

    has = {step: (chain + step >= 0) & (chain + step < total) for step in (-2, -1, 1, 2)}
    eye = iota((56, 128), 0) == iota((56, 128), 1)

    def turn(matrix, vector):
        column = jnp.sum(matrix * vector, axis=1, keepdims=True)
        return jnp.sum(jnp.where(eye, column, 0.0), axis=0, keepdims=True)

    def lift(column):
        line = jnp.sum(bt_ref[...] * column, axis=0, keepdims=True)
        return jnp.concatenate(
            [line[:, e * WIDE : (e + 1) * WIDE] for e in range(EL)], axis=0
        )

    def gram(a, b):
        prod = a * b
        prod = prod[:, 0:128] + prod[:, 128:256] + prod[:, 256:384]
        return jnp.sum(prod, axis=0, keepdims=True)

    pad_row = jnp.zeros((1, 256), F32)
    residuals, preconds = [rhs], []
    products = {}
    all_copies = []
    for k in range(3):
        res = residuals[k]
        scaled = res / diagonal
        acc = jnp.zeros((NB, WIDE), F32)
        for e in range(EL):
            acc = acc + element(cz_ref, e) * res[e : e + 1, :]
        acc = acc[:, 0:128] + acc[:, 128:256] + acc[:, 256:384]
        first = lift(jnp.sum(acc, axis=1, keepdims=True))
        fl = left_face(first[0:1])
        fr = right_face(first[EL - 1 : EL])
        el = left_face(scaled[0:1]) + fl
        er = right_face(scaled[EL - 1 : EL]) + fr
        f_src[k] = jnp.concatenate([fl, fr, el, er, jnp.zeros((4, 128), F32)], axis=0)
        copies = [
            send(f_src.at[k], f_dst.at[k, i], f_sem, 4 * k + i, chain_peer(step))
            for i, step in ((2, -2), (3, 2), (0, -1), (1, 1))
        ]
        for i in range(k + 1):
            for j in range(k):
                if (i, j) not in products:
                    products[i, j] = gram(residuals[i], preconds[j])
        partial = scaled + first
        if k == 0:
            for copy in g_copies:
                copy.wait()
        for copy in copies:
            copy.wait()
        after1 = jnp.where(has[1], f_dst[k, 0], 0.0)
        before1 = jnp.where(has[-1], f_dst[k, 1], 0.0)
        after2 = jnp.where(has[2], f_dst[k, 2], 0.0)
        before2 = jnp.where(has[-2], f_dst[k, 3], 0.0)
        own_v = before1[1:2] + pltpu.roll(after1[0:1], 64, 1)
        after_v = fr + pltpu.roll(after2[0:1], 64, 1)
        before_v = before2[1:2] + pltpu.roll(fl, 64, 1)
        pre = partial + lift(jnp.sum(w * own_v, axis=1, keepdims=True))
        after_face = jnp.where(has[1], after1[2:3] + turn(g_dst[0], after_v), 0.0)
        before_face = jnp.where(has[-1], before1[3:4] + turn(g_dst[1], before_v), 0.0)
        hi, lo = split2(pre)
        both = jnp.concatenate([hi.astype(F32), lo.astype(F32)], axis=0).astype(BF16)
        stiff = dot(both, kel)
        stiff = stiff[0:EL] + stiff[EL : 2 * EL]
        from_left = pltpu.roll(pltpu.roll(pre, 1, 0), WIDE - NODES + FACE, 1)
        from_left = jnp.where(
            el_row == 0, jnp.concatenate([before_face, pad_row], axis=1), from_left
        )
        from_right = pltpu.roll(pltpu.roll(pre, EL - 1, 0), NODES - FACE, 1)
        from_right = jnp.where(
            el_row == EL - 1,
            jnp.concatenate([pad_row, pltpu.roll(after_face, 38, 1)], axis=1),
            from_right,
        )
        image = conduct * stiff + (RELAX + facew) * pre
        image = image - PENALTY * (
            jnp.where(left, from_left, 0.0) + jnp.where(right, from_right, 0.0)
        )
        preconds.append(pre)
        residuals.append(image - SHIFT * res)

    for i in range(4):
        for j in range(3):
            if (i, j) not in products:
                products[i, j] = gram(residuals[i], preconds[j])
    share = jnp.concatenate(
        [products[i, j] for i in range(4) for j in range(3)] + [jnp.zeros((4, 128), F32)], axis=0
    )
    half = iota((8, 128), 1) < 64
    share = share + pltpu.roll(share, 64, 1)
    share = jnp.where(half, share[0:8], share[8:16])
    at = 0
    stages = (
        [core_peer],
        [plane_peer(i, j) for i, j in plane],
        [z_peer(i) for i in far],
    )
    for stage, to in enumerate(stages):
        s_src[stage] = share
        copies = [
            send(s_src.at[stage], s_dst.at[at + i], s_sem, at + i, peer)
            for i, peer in enumerate(to)
        ]
        for copy in copies:
            copy.wait()
        for i in range(len(to)):
            share = share + s_dst[at + i]
        at += len(to)

    sums = jnp.concatenate(
        [
            jnp.sum(jnp.where(half, share, 0.0), axis=1, keepdims=True),
            jnp.sum(jnp.where(half, 0.0, share), axis=1, keepdims=True),
        ],
        axis=0,
    )
    n = [[sums[3 * i + j : 3 * i + j + 1] for j in range(3)] for i in range(4)]

    def form(p, q):
        value = 0.0
        for i, a in enumerate(p):
            line = 0.0
            for j, b in enumerate(q):
                line = line + n[i][j] * b
            value = value + a * line
        return value

    zero = jnp.zeros((1, 1), F32)
    one = jnp.ones((1, 1), F32)
    res_c = [one]
    dir_c = [one]
    sol_c = [zero, zero, zero]
    inner = form(res_c, res_c)
    for k in range(3):
        image_c = [zero] + dir_c
        image_c = [v + SHIFT * u for v, u in zip(image_c, dir_c + [zero])]
        step = inner / form(image_c, dir_c)
        for j, v in enumerate(dir_c):
            sol_c[j] = sol_c[j] + step * v
        res_c = [u - step * v for u, v in zip(res_c + [zero], image_c)]
        if k < 2:
            fresh = form(res_c, res_c)
            ratio = fresh / inner
            dir_c = [u + ratio * v for u, v in zip(res_c, dir_c + [zero])]
            inner = fresh
    answer = sum(sol_c[j] * preconds[j] for j in range(3))
    remain = sum(res_c[j] * residuals[j] for j in range(4))
    x_out[...] = answer[:, :NODES]
    r_out[...] = remain[:, :NODES]


def on_device(slabs, subs, source, conductivity, basis, values, elements, owners, counts):
    rows = values.shape[0]
    zn = subs // XN
    kel = stencil_constants()
    vmem = pl.BlockSpec(memory_space=pltpu.VMEM)
    hbm = pl.BlockSpec(memory_space=pltpu.HBM)
    slot = zn * CAP
    peers = XN * (slabs // 2) - 1 + 1 + zn - 1
    dma = pltpu.SemaphoreType.DMA
    out = jax.ShapeDtypeStruct(source.shape, F32)
    return pl.pallas_call(
        functools.partial(kernel, slabs, subs),
        out_shape=(out, out),
        in_specs=[hbm] * 8,
        out_specs=(vmem, vmem),
        scratch_shapes=[
            pltpu.SMEM((EL,), F32),
            pltpu.SMEM((1,), jnp.int32),
            pltpu.VMEM((EL, NODES), F32),
            pltpu.VMEM((NB, EL, NODES), F32),
            pltpu.VMEM((NODES, rows), BF16),
            pltpu.VMEM((1, rows), jnp.int32),
            pltpu.VMEM((1, rows), jnp.int32),
            pltpu.VMEM((WIDE, WIDE), BF16),
            pltpu.VMEM((XN, slot, WIDE), BF16),
            pltpu.VMEM((XN, slot, WIDE), BF16),
            pltpu.VMEM((zn, EL, WIDE), F32),
            pltpu.VMEM((zn, EL, WIDE), F32),
            pltpu.VMEM((NB, EL * WIDE), F32),
            pltpu.VMEM((NB, EL * WIDE), F32),
            pltpu.VMEM((3, NB * EL, 128), F32),
            pltpu.VMEM((EL, WIDE), F32),
            pltpu.VMEM((2, 56, 128), F32),
            pltpu.VMEM((2, 56, 128), F32),
            pltpu.VMEM((3, 8, 128), F32),
            pltpu.VMEM((3, 4, 8, 128), F32),
            pltpu.VMEM((3, 8, 128), F32),
            pltpu.VMEM((peers, 8, 128), F32),
            dma((2, XN)),
            dma((2, zn)),
            dma((2, 2)),
            dma((2, 12)),
            dma((2, peers)),
            dma((8,)),
        ],
        compiler_params=pltpu.CompilerParams(
            collective_id=0, has_side_effects=True, vmem_limit_bytes=60 * 1024 * 1024
        ),
    )(
        conductivity,
        counts,
        source,
        basis,
        values.T,
        elements.reshape(1, rows),
        owners.reshape(1, rows),
        jnp.asarray(kel, BF16),
    )


def solution(mesh):
    both = ("slab", "sub")
    placed = (
        P(both, None),
        P(both),
        P(None, both, None),
        P(both, None),
        P(both),
        P(both, None),
        P(both),
    )
    return jax.shard_map(
        functools.partial(on_device, mesh.shape["slab"], mesh.shape["sub"]),
        mesh=mesh,
        in_specs=placed,
        out_specs=(P(both, None), P(both, None)),
        check_vma=False,
    )
```

```python
import functools

import jax
import jax.numpy as jnp
import numpy as np
from jax import lax
from jax.experimental import pallas as pl
from jax.experimental.pallas import tpu as pltpu
from jax.sharding import PartitionSpec as P

BLOCK = 128
CAP = 6
NODES = 343
WIDE = 384
FACE = 49
EL = 8
NB = 64
XN = 4
MARK = 120
EARLY = 24
SHIFT = 1.0
PENALTY = 10.0
RELAX = 0.2
HIGH = lax.Precision.HIGHEST
F32 = jnp.float32
BF16 = jnp.bfloat16
NT = (((1,), (1,)), ((), ()))
TN = (((0,), (0,)), ((), ()))


def stencil_constants():
    second = np.diag(np.array([1.0, 2, 2, 2, 2, 2, 1]))
    for i in range(6):
        second[i, i + 1] = second[i + 1, i] = -1.0
    one = np.eye(7)
    kel = (
        np.kron(np.kron(second, one), one)
        + np.kron(np.kron(one, second), one)
        + np.kron(one, np.kron(one, second))
    )
    full = np.zeros((WIDE, WIDE), np.float32)
    full[:NODES, :NODES] = kel
    full[NODES + 1] = np.diagonal(full)
    return full


def split2(value):
    hi = value.astype(BF16)
    lo = (value - hi.astype(F32)).astype(BF16)
    return hi, lo


def iota(shape, dim):
    return lax.broadcasted_iota(jnp.int32, shape, dim)


def dot(a, b, dims=(((1,), (0,)), ((), ())), precision=None):
    return lax.dot_general(a, b, dims, precision=precision, preferred_element_type=F32)


def kernel(
    slabs,
    subs,
    cond_ref,
    count_ref,
    src_ref,
    basis_ref,
    vals_ref,
    elem_ref,
    own_ref,
    kel_ref,
    out_ref,
    cond_in,
    count_in,
    src_in,
    basis_in,
    vals_in,
    elem_in,
    own_in,
    kel_in,
    a_src,
    a_dst,
    b_src,
    b_dst,
    bt_ref,
    cz_ref,
    padded,
    source_ref,
    g_src,
    g_dst,
    f_src,
    f_dst,
    s_src,
    s_dst,
    a_sem,
    b_sem,
    g_sem,
    f_sem,
    s_sem,
    in_sem,
    relay_sem,
):
    zn = subs // XN
    total = slabs * subs
    slab = lax.axis_index("slab")
    sub = lax.axis_index("sub")
    x = lax.rem(sub, XN)
    z = lax.div(sub, XN)
    chain = slab * subs + sub
    rows = vals_ref.shape[1]
    slot = zn * CAP

    def x_peer(i):
        return (slab, z * XN + lax.rem(x + i, XN))

    def z_peer(i):
        return (slab, lax.rem(z + i, zn) * XN + x)

    def plane_peer(i, j):
        return (lax.rem(slab + 2 * j, slabs), z * XN + lax.rem(x + i, XN))

    core_peer = (slab + 1 - 2 * lax.rem(slab, 2), sub)
    ys = slabs // 2
    far = sorted(range(1, zn), key=lambda i: -min(i, zn - i))
    plane = [(i, j) for i in range(XN) for j in range(ys) if i or j]
    plane.sort(key=lambda p: -min(p[0], XN - p[0]) - min(p[1], ys - p[1]))
    x_order = sorted(range(1, XN), key=lambda i: -min(i, XN - i))

    def chain_peer(step):
        other = lax.rem(chain + step + total, total)
        return (lax.div(other, subs), lax.rem(other, subs))

    reach = min(4, zn // 2)
    peers = (
        [z_peer(i) for i in far if min(i, zn - i) <= reach]
        + [chain_peer(step) for step in (-2, 2, -1, 1)]
        + [plane_peer(i, j) for i, j in plane]
        + [core_peer]
    )
    barrier = pltpu.get_barrier_semaphore()
    for peer in peers:
        pl.semaphore_signal(
            barrier, inc=1, device_id=peer, device_id_type=pl.DeviceIdType.MESH
        )

    def send(src, dst, sems, k, peer):
        copy = pltpu.make_async_remote_copy(
            src_ref=src,
            dst_ref=dst,
            send_sem=sems.at[0, k],
            recv_sem=sems.at[1, k],
            device_id=peer,
            device_id_type=pl.DeviceIdType.MESH,
        )
        copy.start()
        return copy

    fetches = [
        pltpu.make_async_copy(src, dst, in_sem.at[k])
        for k, (src, dst) in enumerate(
            (
                (own_ref, own_in),
                (count_ref, count_in),
                (elem_ref, elem_in),
                (vals_ref, vals_in),
                (basis_ref, basis_in),
                (kel_ref, kel_in),
                (cond_ref, cond_in),
                (src_ref, src_in),
            )
        )
    ]
    for fetch in fetches:
        fetch.start()

    for fetch in fetches[:4]:
        fetch.wait()
    order = iota((subs, rows), 0)
    order = lax.rem(order, zn) * XN + lax.div(order, zn)
    live = lax.div(iota((subs, rows), 1), BLOCK) < count_in[0]
    owned = ((own_in[...] == order) & live).astype(F32)
    before = (iota((rows, rows), 0) < iota((rows, rows), 1)).astype(BF16)
    rank = dot(owned.astype(BF16), before)
    pieces = []
    for to in range(XN):
        mine = owned[to * zn : (to + 1) * zn]
        place = rank[to * zn : (to + 1) * zn]
        for j in range(CAP):
            pieces.append(jnp.where(place == float(j), mine, 0.0))
    select = jnp.concatenate(pieces, axis=0).astype(BF16)
    marks = (elem_in[...] == iota((128, rows), 0) - MARK).astype(BF16)
    moved = dot(select, vals_in[...], NT).astype(BF16)
    marked = dot(select, marks, NT).astype(BF16)
    a_src[:, :, :256] = moved[:, :256].reshape(XN, slot, 256)
    a_src[:, :, 256:] = marked.reshape(XN, slot, 128)
    a_src[:, :, 256:NODES] = moved[:, 256:].reshape(XN, slot, NODES - 256)

    pl.semaphore_wait(barrier, len(peers))
    relays = [z_peer(reach), z_peer(zn - reach)] if zn // 2 > reach else []
    for peer in relays:
        pl.semaphore_signal(
            relay_sem, inc=1, device_id=peer, device_id_type=pl.DeviceIdType.MESH
        )
    a_copies = [
        send(a_src.at[lax.rem(x + i, XN)], a_dst.at[i], a_sem, i, x_peer(i))
        for i in x_order
    ]
    a_dst[0] = a_src[x]

    for fetch in fetches[4:]:
        fetch.wait()
    lane = iota((1, WIDE), 1)
    left = lane < FACE
    right = (lane >= NODES - FACE) & (lane < NODES)
    facew = jnp.where(left | right, PENALTY, 0.0)
    flat = basis_in[...].reshape(NB * EL, NODES)
    padded[2] = jnp.zeros((NB * EL, 128), F32)
    padded[0] = flat[:, 0:128]
    padded[1] = flat[:, 128:256]
    padded[2, :, : NODES - 256] = flat[:, 256:]
    for t in range(3):
        for e in range(EL):
            at = e * WIDE + t * 128
            bt_ref[:, at : at + 128] = padded[t, pl.ds(e, NB, stride=EL), :]

    def element(ref, e):
        return ref[:, e * WIDE : (e + 1) * WIDE]

    kel = kel_in[...]
    applied = []
    for e in range(EL):
        be = element(bt_ref, e)
        hi, lo = split2(be)
        stiff = dot(hi, kel) + dot(lo, kel)
        out = cond_in[e] * stiff + (RELAX + facew) * be
        if e > 0:
            turned = pltpu.roll(element(bt_ref, e - 1), WIDE - NODES + FACE, 1)
            out = out - jnp.where(left, PENALTY * turned, 0.0)
        if e < EL - 1:
            turned = pltpu.roll(element(bt_ref, e + 1), NODES - FACE, 1)
            out = out - jnp.where(right, PENALTY * turned, 0.0)
        applied.append(out)
    matrix = dot(bt_ref[...], jnp.concatenate(applied, axis=1), NT, HIGH)

    unit = (iota((NB, NB), 0) == iota((NB, NB), 1)).astype(F32)
    work = jnp.concatenate([matrix, unit], axis=1)
    row_id = iota((NB, 2 * NB), 0)

    def eliminate(work, k):
        row = work[k : k + 1, :] / work[k : k + 1, k : k + 1]
        return jnp.where(row_id == k, row, work - work[:, k : k + 1] * row)

    for k in range(EARLY):
        work = eliminate(work, k)

    for copy in a_copies:
        copy.wait()
    arrived = a_dst[...].reshape(XN * slot, WIDE)
    spread = (iota((128, 128), 0) == MARK + lax.rem(iota((128, 128), 1), EL)).astype(BF16)
    spread = dot(arrived[:, 256:], spread)
    keep = lax.rem(iota(spread.shape, 0), zn) == lax.div(iota(spread.shape, 1), EL)
    weights = jnp.where(keep, spread, 0.0)
    sums = dot(weights.T.astype(BF16), arrived)
    if relays:
        pl.semaphore_wait(relay_sem, len(relays))
    b_src[...] = sums[: zn * EL].reshape(zn, EL, WIDE)
    b_copies = [
        send(b_src.at[lax.rem(z + i, zn)], b_dst.at[i], b_sem, i, z_peer(i))
        for i in far
    ]
    b_dst[0] = b_src[z]

    for k in range(EARLY, NB):
        work = eliminate(work, k)
    inverse = work[:, NB:]
    cz_ref[...] = dot(inverse, bt_ref[...], precision=HIGH)

    low = iota((1, 128), 1)
    near = low < FACE

    def left_face(value):
        return jnp.where(near, value[:, 0:128], 0.0)

    def right_face(value):
        return jnp.where(near, pltpu.roll(value[:, 256:WIDE], 128 - 38, 1), 0.0)

    w = PENALTY * (
        left_face(element(cz_ref, 0))
        + pltpu.roll(right_face(element(cz_ref, EL - 1)), 64, 1)
    )
    face_l = left_face(element(bt_ref, 0))
    face_r = right_face(element(bt_ref, EL - 1))
    g_src[0] = dot(face_l.T, w, precision=HIGH)[:56]
    g_src[1] = dot(face_r.T, w, precision=HIGH)[:56]
    g_copies = [
        send(g_src.at[0], g_dst.at[0], g_sem, 0, chain_peer(-1)),
        send(g_src.at[1], g_dst.at[1], g_sem, 1, chain_peer(1)),
    ]

    el_row = iota((EL, WIDE), 0)
    conduct = jnp.zeros((EL, WIDE), F32)
    for e in range(EL):
        conduct = jnp.where(el_row == e, cond_in[e], conduct)
    kdiag = kel_in[NODES - 7 : NODES + 9].astype(F32)[8:9]
    diagonal = conduct * kdiag + RELAX + facew
    inner_lane = iota((EL, WIDE), 1) < NODES
    source_ref[:, 256:] = jnp.zeros((EL, 128), F32)
    source_ref[:, :NODES] = src_in[...]
    for copy in b_copies:
        copy.wait()
    currents = b_dst[0]
    for i in range(1, zn):
        currents = currents + b_dst[i]
    rhs = source_ref[...] + jnp.where(inner_lane, currents, 0.0)

    has = {step: (chain + step >= 0) & (chain + step < total) for step in (-2, -1, 1, 2)}
    eye = iota((56, 128), 0) == iota((56, 128), 1)

    def turn(matrix, vector):
        column = jnp.sum(matrix * vector, axis=1, keepdims=True)
        return jnp.sum(jnp.where(eye, column, 0.0), axis=0, keepdims=True)

    def lift(column):
        line = jnp.sum(bt_ref[...] * column, axis=0, keepdims=True)
        return jnp.concatenate(
            [line[:, e * WIDE : (e + 1) * WIDE] for e in range(EL)], axis=0
        )

    def gram(a, b):
        prod = a * b
        prod = prod[:, 0:128] + prod[:, 128:256] + prod[:, 256:384]
        return jnp.sum(prod, axis=0, keepdims=True)

    pad_row = jnp.zeros((1, 256), F32)
    residuals, preconds = [rhs], []
    products = {}
    all_copies = []
    for k in range(3):
        res = residuals[k]
        scaled = res / diagonal
        acc = jnp.zeros((NB, WIDE), F32)
        for e in range(EL):
            acc = acc + element(cz_ref, e) * res[e : e + 1, :]
        acc = acc[:, 0:128] + acc[:, 128:256] + acc[:, 256:384]
        first = lift(jnp.sum(acc, axis=1, keepdims=True))
        fl = left_face(first[0:1])
        fr = right_face(first[EL - 1 : EL])
        el = left_face(scaled[0:1]) + fl
        er = right_face(scaled[EL - 1 : EL]) + fr
        f_src[k] = jnp.concatenate([fl, fr, el, er, jnp.zeros((4, 128), F32)], axis=0)
        copies = [
            send(f_src.at[k], f_dst.at[k, i], f_sem, 4 * k + i, chain_peer(step))
            for i, step in ((2, -2), (3, 2), (0, -1), (1, 1))
        ]
        for i in range(k + 1):
            for j in range(k):
                if (i, j) not in products:
                    products[i, j] = gram(residuals[i], preconds[j])
        partial = scaled + first
        if k == 0:
            for copy in g_copies:
                copy.wait()
        for copy in copies:
            copy.wait()
        after1 = jnp.where(has[1], f_dst[k, 0], 0.0)
        before1 = jnp.where(has[-1], f_dst[k, 1], 0.0)
        after2 = jnp.where(has[2], f_dst[k, 2], 0.0)
        before2 = jnp.where(has[-2], f_dst[k, 3], 0.0)
        own_v = before1[1:2] + pltpu.roll(after1[0:1], 64, 1)
        after_v = fr + pltpu.roll(after2[0:1], 64, 1)
        before_v = before2[1:2] + pltpu.roll(fl, 64, 1)
        pre = partial + lift(jnp.sum(w * own_v, axis=1, keepdims=True))
        after_face = jnp.where(has[1], after1[2:3] + turn(g_dst[0], after_v), 0.0)
        before_face = jnp.where(has[-1], before1[3:4] + turn(g_dst[1], before_v), 0.0)
        hi, lo = split2(pre)
        both = jnp.concatenate([hi.astype(F32), lo.astype(F32)], axis=0).astype(BF16)
        stiff = dot(both, kel)
        stiff = stiff[0:EL] + stiff[EL : 2 * EL]
        from_left = pltpu.roll(pltpu.roll(pre, 1, 0), WIDE - NODES + FACE, 1)
        from_left = jnp.where(
            el_row == 0, jnp.concatenate([before_face, pad_row], axis=1), from_left
        )
        from_right = pltpu.roll(pltpu.roll(pre, EL - 1, 0), NODES - FACE, 1)
        from_right = jnp.where(
            el_row == EL - 1,
            jnp.concatenate([pad_row, pltpu.roll(after_face, 38, 1)], axis=1),
            from_right,
        )
        image = conduct * stiff + (RELAX + facew) * pre
        image = image - PENALTY * (
            jnp.where(left, from_left, 0.0) + jnp.where(right, from_right, 0.0)
        )
        preconds.append(pre)
        residuals.append(image - SHIFT * res)

    for i in range(4):
        for j in range(3):
            if (i, j) not in products:
                products[i, j] = gram(residuals[i], preconds[j])
    share = jnp.concatenate(
        [products[i, j] for i in range(4) for j in range(3)] + [jnp.zeros((4, 128), F32)], axis=0
    )
    half = iota((8, 128), 1) < 64
    share = share + pltpu.roll(share, 64, 1)
    share = jnp.where(half, share[0:8], share[8:16])
    at = 0
    stages = (
        [core_peer],
        [plane_peer(i, j) for i, j in plane],
        [z_peer(i) for i in far],
    )
    for stage, to in enumerate(stages):
        s_src[stage] = share
        copies = [
            send(s_src.at[stage], s_dst.at[at + i], s_sem, at + i, peer)
            for i, peer in enumerate(to)
        ]
        for copy in copies:
            copy.wait()
        for i in range(len(to)):
            share = share + s_dst[at + i]
        at += len(to)

    sums = jnp.concatenate(
        [
            jnp.sum(jnp.where(half, share, 0.0), axis=1, keepdims=True),
            jnp.sum(jnp.where(half, 0.0, share), axis=1, keepdims=True),
        ],
        axis=0,
    )
    n = [[sums[3 * i + j : 3 * i + j + 1] for j in range(3)] for i in range(4)]

    def form(p, q):
        value = 0.0
        for i, a in enumerate(p):
            line = 0.0
            for j, b in enumerate(q):
                line = line + n[i][j] * b
            value = value + a * line
        return value

    zero = jnp.zeros((1, 1), F32)
    one = jnp.ones((1, 1), F32)
    res_c = [one]
    dir_c = [one]
    sol_c = [zero, zero, zero]
    inner = form(res_c, res_c)
    for k in range(3):
        image_c = [zero] + dir_c
        image_c = [v + SHIFT * u for v, u in zip(image_c, dir_c + [zero])]
        step = inner / form(image_c, dir_c)
        for j, v in enumerate(dir_c):
            sol_c[j] = sol_c[j] + step * v
        res_c = [u - step * v for u, v in zip(res_c + [zero], image_c)]
        if k < 2:
            fresh = form(res_c, res_c)
            ratio = fresh / inner
            dir_c = [u + ratio * v for u, v in zip(res_c, dir_c + [zero])]
            inner = fresh
    answer = sum(sol_c[j] * preconds[j] for j in range(3))
    remain = sum(res_c[j] * residuals[j] for j in range(4))
    out_ref[0] = answer
    out_ref[1] = remain


def on_device(slabs, subs, source, conductivity, basis, values, elements, owners, counts):
    rows = values.shape[0]
    zn = subs // XN
    kel = stencil_constants()
    vmem = pl.BlockSpec(memory_space=pltpu.VMEM)
    hbm = pl.BlockSpec(memory_space=pltpu.HBM)
    slot = zn * CAP
    peers = XN * (slabs // 2) - 1 + 1 + zn - 1
    dma = pltpu.SemaphoreType.DMA
    out = jax.ShapeDtypeStruct((2, EL, WIDE), F32)
    both = pl.pallas_call(
        functools.partial(kernel, slabs, subs),
        out_shape=out,
        in_specs=[hbm] * 8,
        out_specs=vmem,
        scratch_shapes=[
            pltpu.SMEM((EL,), F32),
            pltpu.SMEM((1,), jnp.int32),
            pltpu.VMEM((EL, NODES), F32),
            pltpu.VMEM((NB, EL, NODES), F32),
            pltpu.VMEM((NODES, rows), BF16),
            pltpu.VMEM((1, rows), jnp.int32),
            pltpu.VMEM((1, rows), jnp.int32),
            pltpu.VMEM((WIDE, WIDE), BF16),
            pltpu.VMEM((XN, slot, WIDE), BF16),
            pltpu.VMEM((XN, slot, WIDE), BF16),
            pltpu.VMEM((zn, EL, WIDE), F32),
            pltpu.VMEM((zn, EL, WIDE), F32),
            pltpu.VMEM((NB, EL * WIDE), F32),
            pltpu.VMEM((NB, EL * WIDE), F32),
            pltpu.VMEM((3, NB * EL, 128), F32),
            pltpu.VMEM((EL, WIDE), F32),
            pltpu.VMEM((2, 56, 128), F32),
            pltpu.VMEM((2, 56, 128), F32),
            pltpu.VMEM((3, 8, 128), F32),
            pltpu.VMEM((3, 4, 8, 128), F32),
            pltpu.VMEM((3, 8, 128), F32),
            pltpu.VMEM((peers, 8, 128), F32),
            dma((2, XN)),
            dma((2, zn)),
            dma((2, 2)),
            dma((2, 12)),
            dma((2, peers)),
            dma((8,)),
            pltpu.SemaphoreType.REGULAR,
        ],
        compiler_params=pltpu.CompilerParams(
            collective_id=0, has_side_effects=True, vmem_limit_bytes=60 * 1024 * 1024
        ),
    )(
        conductivity,
        counts,
        source,
        basis,
        values.T,
        elements.reshape(1, rows),
        owners.reshape(1, rows),
        jnp.asarray(kel, BF16),
    )
    return both[0, :, :NODES], both[1, :, :NODES]


def solution(mesh):
    both = ("slab", "sub")
    placed = (
        P(both, None),
        P(both),
        P(None, both, None),
        P(both, None),
        P(both),
        P(both, None),
        P(both),
    )
    return jax.shard_map(
        functools.partial(on_device, mesh.shape["slab"], mesh.shape["sub"]),
        mesh=mesh,
        in_specs=placed,
        out_specs=(P(both, None), P(both, None)),
        check_vma=False,
    )
```

```python
import functools

import jax
import jax.numpy as jnp
import numpy as np
from jax import lax
from jax.experimental import pallas as pl
from jax.experimental.pallas import tpu as pltpu
from jax.sharding import PartitionSpec as P

BLOCK = 128
CAP = 6
NODES = 343
WIDE = 384
FACE = 49
EL = 8
NB = 64
XN = 4
MARK = 120
EARLY = 24
SHIFT = 1.0
PENALTY = 10.0
RELAX = 0.2
HIGH = lax.Precision.HIGHEST
F32 = jnp.float32
BF16 = jnp.bfloat16
NT = (((1,), (1,)), ((), ()))
TN = (((0,), (0,)), ((), ()))


def stencil_constants():
    second = np.diag(np.array([1.0, 2, 2, 2, 2, 2, 1]))
    for i in range(6):
        second[i, i + 1] = second[i + 1, i] = -1.0
    one = np.eye(7)
    kel = (
        np.kron(np.kron(second, one), one)
        + np.kron(np.kron(one, second), one)
        + np.kron(one, np.kron(one, second))
    )
    full = np.zeros((WIDE, WIDE), np.float32)
    full[:NODES, :NODES] = kel
    full[NODES + 1] = np.diagonal(full)
    return full


def split2(value):
    hi = value.astype(BF16)
    lo = (value - hi.astype(F32)).astype(BF16)
    return hi, lo


def iota(shape, dim):
    return lax.broadcasted_iota(jnp.int32, shape, dim)


def dot(a, b, dims=(((1,), (0,)), ((), ())), precision=None):
    return lax.dot_general(a, b, dims, precision=precision, preferred_element_type=F32)


def kernel(
    slabs,
    subs,
    cond_ref,
    count_ref,
    src_ref,
    basis_ref,
    vals_ref,
    elem_ref,
    own_ref,
    kel_ref,
    out_ref,
    cond_in,
    count_in,
    src_in,
    basis_in,
    vals_in,
    elem_in,
    own_in,
    kel_in,
    a_src,
    a_dst,
    b_src,
    b_dst,
    bt_ref,
    cz_ref,
    padded,
    source_ref,
    g_src,
    g_dst,
    f_src,
    f_dst,
    s_src,
    s_dst,
    a_sem,
    b_sem,
    g_sem,
    f_sem,
    s_sem,
    in_sem,
    relay_sem,
):
    zn = subs // XN
    total = slabs * subs
    slab = lax.axis_index("slab")
    sub = lax.axis_index("sub")
    x = lax.rem(sub, XN)
    z = lax.div(sub, XN)
    chain = slab * subs + sub
    rows = vals_ref.shape[1]
    slot = zn * CAP

    def x_peer(i):
        return (slab, z * XN + lax.rem(x + i, XN))

    def z_peer(i):
        return (slab, lax.rem(z + i, zn) * XN + x)

    def plane_peer(i, j):
        return (lax.rem(slab + 2 * j, slabs), z * XN + lax.rem(x + i, XN))

    core_peer = (slab + 1 - 2 * lax.rem(slab, 2), sub)
    ys = slabs // 2
    far = sorted(range(1, zn), key=lambda i: -min(i, zn - i))
    plane = [(i, j) for i in range(XN) for j in range(ys) if i or j]
    plane.sort(key=lambda p: -min(p[0], XN - p[0]) - min(p[1], ys - p[1]))
    x_order = sorted(range(1, XN), key=lambda i: -min(i, XN - i))

    def chain_peer(step):
        other = lax.rem(chain + step + total, total)
        return (lax.div(other, subs), lax.rem(other, subs))

    reach = min(4, zn // 2)
    peers = (
        [z_peer(i) for i in far if min(i, zn - i) <= reach]
        + [(lax.rem(slab + i, slabs), sub) for i in range(1, slabs)]
        + [x_peer(i) for i in x_order]
    )
    barrier = pltpu.get_barrier_semaphore()
    for peer in peers:
        pl.semaphore_signal(
            barrier, inc=1, device_id=peer, device_id_type=pl.DeviceIdType.MESH
        )

    def send(src, dst, sems, k, peer):
        copy = pltpu.make_async_remote_copy(
            src_ref=src,
            dst_ref=dst,
            send_sem=sems.at[0, k],
            recv_sem=sems.at[1, k],
            device_id=peer,
            device_id_type=pl.DeviceIdType.MESH,
        )
        copy.start()
        return copy

    fetches = [
        pltpu.make_async_copy(src, dst, in_sem.at[k])
        for k, (src, dst) in enumerate(
            (
                (own_ref, own_in),
                (count_ref, count_in),
                (elem_ref, elem_in),
                (vals_ref, vals_in),
                (basis_ref, basis_in),
                (kel_ref, kel_in),
                (cond_ref, cond_in),
                (src_ref, src_in),
            )
        )
    ]
    for fetch in fetches:
        fetch.start()

    leaving = []

    def settle():
        while leaving:
            leaving.pop(0).wait_send()

    for fetch in fetches[:4]:
        fetch.wait()
    order = iota((subs, rows), 0)
    order = lax.rem(order, zn) * XN + lax.div(order, zn)
    live = lax.div(iota((subs, rows), 1), BLOCK) < count_in[0]
    owned = ((own_in[...] == order) & live).astype(F32)
    before = (iota((rows, rows), 0) < iota((rows, rows), 1)).astype(BF16)
    rank = dot(owned.astype(BF16), before)
    pieces = []
    for to in range(XN):
        mine = owned[to * zn : (to + 1) * zn]
        place = rank[to * zn : (to + 1) * zn]
        for j in range(CAP):
            pieces.append(jnp.where(place == float(j), mine, 0.0))
    select = jnp.concatenate(pieces, axis=0).astype(BF16)
    marks = (elem_in[...] == iota((128, rows), 0) - MARK).astype(BF16)
    moved = dot(select, vals_in[...], NT).astype(BF16)
    marked = dot(select, marks, NT).astype(BF16)
    a_src[:, :, :256] = moved[:, :256].reshape(XN, slot, 256)
    a_src[:, :, 256:] = marked.reshape(XN, slot, 128)
    a_src[:, :, 256:NODES] = moved[:, 256:].reshape(XN, slot, NODES - 256)

    pl.semaphore_wait(barrier, len(peers))
    relays = [z_peer(reach), z_peer(zn - reach)] if zn // 2 > reach else []
    for peer in relays:
        pl.semaphore_signal(
            relay_sem, inc=1, device_id=peer, device_id_type=pl.DeviceIdType.MESH
        )
    a_copies = [
        send(a_src.at[lax.rem(x + i, XN)], a_dst.at[i], a_sem, i, x_peer(i))
        for i in x_order
    ]
    a_dst[0] = a_src[x]

    for fetch in fetches[4:]:
        fetch.wait()
    lane = iota((1, WIDE), 1)
    left = lane < FACE
    right = (lane >= NODES - FACE) & (lane < NODES)
    facew = jnp.where(left | right, PENALTY, 0.0)
    flat = basis_in[...].reshape(NB * EL, NODES)
    padded[2] = jnp.zeros((NB * EL, 128), F32)
    padded[0] = flat[:, 0:128]
    padded[1] = flat[:, 128:256]
    padded[2, :, : NODES - 256] = flat[:, 256:]
    for t in range(3):
        for e in range(EL):
            at = e * WIDE + t * 128
            bt_ref[:, at : at + 128] = padded[t, pl.ds(e, NB, stride=EL), :]

    def element(ref, e):
        return ref[:, e * WIDE : (e + 1) * WIDE]

    kel = kel_in[...]
    applied = []
    for e in range(EL):
        be = element(bt_ref, e)
        hi, lo = split2(be)
        stiff = dot(hi, kel) + dot(lo, kel)
        out = cond_in[e] * stiff + (RELAX + facew) * be
        if e > 0:
            turned = pltpu.roll(element(bt_ref, e - 1), WIDE - NODES + FACE, 1)
            out = out - jnp.where(left, PENALTY * turned, 0.0)
        if e < EL - 1:
            turned = pltpu.roll(element(bt_ref, e + 1), NODES - FACE, 1)
            out = out - jnp.where(right, PENALTY * turned, 0.0)
        applied.append(out)
    matrix = dot(bt_ref[...], jnp.concatenate(applied, axis=1), NT, HIGH)

    unit = (iota((NB, NB), 0) == iota((NB, NB), 1)).astype(F32)
    work = jnp.concatenate([matrix, unit], axis=1)
    row_id = iota((NB, 2 * NB), 0)

    def eliminate(work, k):
        row = work[k : k + 1, :] / work[k : k + 1, k : k + 1]
        return jnp.where(row_id == k, row, work - work[:, k : k + 1] * row)

    for k in range(EARLY):
        work = eliminate(work, k)

    for copy in a_copies:
        copy.wait_recv()
    arrived = a_dst[...].reshape(XN * slot, WIDE)
    spread = (iota((128, 128), 0) == MARK + lax.rem(iota((128, 128), 1), EL)).astype(BF16)
    spread = dot(arrived[:, 256:], spread)
    keep = lax.rem(iota(spread.shape, 0), zn) == lax.div(iota(spread.shape, 1), EL)
    weights = jnp.where(keep, spread, 0.0)
    sums = dot(weights.T.astype(BF16), arrived)
    if relays:
        pl.semaphore_wait(relay_sem, len(relays))
    b_src[...] = sums[: zn * EL].reshape(zn, EL, WIDE)
    b_copies = [
        send(b_src.at[lax.rem(z + i, zn)], b_dst.at[i], b_sem, i, z_peer(i))
        for i in far
    ]
    b_dst[0] = b_src[z]
    leaving.extend(a_copies)
    settle()

    for k in range(EARLY, NB):
        work = eliminate(work, k)
    inverse = work[:, NB:]
    cz_ref[...] = dot(inverse, bt_ref[...], precision=HIGH)

    low = iota((1, 128), 1)
    near = low < FACE

    def left_face(value):
        return jnp.where(near, value[:, 0:128], 0.0)

    def right_face(value):
        return jnp.where(near, pltpu.roll(value[:, 256:WIDE], 128 - 38, 1), 0.0)

    w = PENALTY * (
        left_face(element(cz_ref, 0))
        + pltpu.roll(right_face(element(cz_ref, EL - 1)), 64, 1)
    )
    face_l = left_face(element(bt_ref, 0))
    face_r = right_face(element(bt_ref, EL - 1))
    g_src[0] = dot(face_l.T, w, precision=HIGH)[:56]
    g_src[1] = dot(face_r.T, w, precision=HIGH)[:56]
    el_row = iota((EL, WIDE), 0)
    conduct = jnp.zeros((EL, WIDE), F32)
    for e in range(EL):
        conduct = jnp.where(el_row == e, cond_in[e], conduct)
    kdiag = kel_in[NODES - 7 : NODES + 9].astype(F32)[8:9]
    diagonal = conduct * kdiag + RELAX + facew
    inner_lane = iota((EL, WIDE), 1) < NODES
    source_ref[:, 256:] = jnp.zeros((EL, 128), F32)
    source_ref[:, :NODES] = src_in[...]
    for copy in b_copies:
        copy.wait_recv()
    g_copies = [
        send(g_src.at[0], g_dst.at[0], g_sem, 0, chain_peer(-1)),
        send(g_src.at[1], g_dst.at[1], g_sem, 1, chain_peer(1)),
    ]
    leaving.extend(b_copies + g_copies)
    currents = b_dst[0]
    for i in range(1, zn):
        currents = currents + b_dst[i]
    rhs = source_ref[...] + jnp.where(inner_lane, currents, 0.0)

    has = {step: (chain + step >= 0) & (chain + step < total) for step in (-2, -1, 1, 2)}
    eye = iota((56, 128), 0) == iota((56, 128), 1)

    def turn(matrix, vector):
        column = jnp.sum(matrix * vector, axis=1, keepdims=True)
        return jnp.sum(jnp.where(eye, column, 0.0), axis=0, keepdims=True)

    def lift(column):
        line = jnp.sum(bt_ref[...] * column, axis=0, keepdims=True)
        return jnp.concatenate(
            [line[:, e * WIDE : (e + 1) * WIDE] for e in range(EL)], axis=0
        )

    def gram(a, b):
        prod = a * b
        prod = prod[:, 0:128] + prod[:, 128:256] + prod[:, 256:384]
        return jnp.sum(prod, axis=0, keepdims=True)

    pad_row = jnp.zeros((1, 256), F32)
    residuals, preconds = [rhs], []
    products = {}
    all_copies = []
    for k in range(3):
        res = residuals[k]
        scaled = res / diagonal
        acc = jnp.zeros((NB, WIDE), F32)
        for e in range(EL):
            acc = acc + element(cz_ref, e) * res[e : e + 1, :]
        acc = acc[:, 0:128] + acc[:, 128:256] + acc[:, 256:384]
        first = lift(jnp.sum(acc, axis=1, keepdims=True))
        fl = left_face(first[0:1])
        fr = right_face(first[EL - 1 : EL])
        el = left_face(scaled[0:1]) + fl
        er = right_face(scaled[EL - 1 : EL]) + fr
        f_src[k] = jnp.concatenate([fl, fr, el, er, jnp.zeros((4, 128), F32)], axis=0)
        copies = [
            send(f_src.at[k], f_dst.at[k, i], f_sem, 4 * k + i, chain_peer(step))
            for i, step in ((2, -2), (3, 2), (0, -1), (1, 1))
        ]
        settle()
        leaving.extend(copies)
        for i in range(k + 1):
            for j in range(k):
                if (i, j) not in products:
                    products[i, j] = gram(residuals[i], preconds[j])
        partial = scaled + first
        for copy in copies[2:]:
            copy.wait_recv()
        after1 = jnp.where(has[1], f_dst[k, 0], 0.0)
        before1 = jnp.where(has[-1], f_dst[k, 1], 0.0)
        own_v = before1[1:2] + pltpu.roll(after1[0:1], 64, 1)
        pre = partial + lift(jnp.sum(w * own_v, axis=1, keepdims=True))
        hi, lo = split2(pre)
        both = jnp.concatenate([hi.astype(F32), lo.astype(F32)], axis=0).astype(BF16)
        stiff = dot(both, kel)
        stiff = stiff[0:EL] + stiff[EL : 2 * EL]
        for copy in copies[:2] + (g_copies if k == 0 else []):
            copy.wait_recv()
        after2 = jnp.where(has[2], f_dst[k, 2], 0.0)
        before2 = jnp.where(has[-2], f_dst[k, 3], 0.0)
        after_v = fr + pltpu.roll(after2[0:1], 64, 1)
        before_v = before2[1:2] + pltpu.roll(fl, 64, 1)
        after_face = jnp.where(has[1], after1[2:3] + turn(g_dst[0], after_v), 0.0)
        before_face = jnp.where(has[-1], before1[3:4] + turn(g_dst[1], before_v), 0.0)
        from_left = pltpu.roll(pltpu.roll(pre, 1, 0), WIDE - NODES + FACE, 1)
        from_left = jnp.where(
            el_row == 0, jnp.concatenate([before_face, pad_row], axis=1), from_left
        )
        from_right = pltpu.roll(pltpu.roll(pre, EL - 1, 0), NODES - FACE, 1)
        from_right = jnp.where(
            el_row == EL - 1,
            jnp.concatenate([pad_row, pltpu.roll(after_face, 38, 1)], axis=1),
            from_right,
        )
        image = conduct * stiff + (RELAX + facew) * pre
        image = image - PENALTY * (
            jnp.where(left, from_left, 0.0) + jnp.where(right, from_right, 0.0)
        )
        preconds.append(pre)
        residuals.append(image - SHIFT * res)

    for i in range(4):
        for j in range(3):
            if (i, j) not in products:
                products[i, j] = gram(residuals[i], preconds[j])
    share = jnp.concatenate(
        [products[i, j] for i in range(4) for j in range(3)] + [jnp.zeros((4, 128), F32)], axis=0
    )
    half = iota((8, 128), 1) < 64
    share = share + pltpu.roll(share, 64, 1)
    share = jnp.where(half, share[0:8], share[8:16])
    at = 0
    stages = (
        [core_peer],
        [plane_peer(i, j) for i, j in plane],
        [z_peer(i) for i in far],
    )
    for stage, to in enumerate(stages):
        s_src[stage] = share
        copies = [
            send(s_src.at[stage], s_dst.at[at + i], s_sem, at + i, peer)
            for i, peer in enumerate(to)
        ]
        settle()
        leaving.extend(copies)
        for copy in copies:
            copy.wait_recv()
        for i in range(len(to)):
            share = share + s_dst[at + i]
        at += len(to)

    sums = jnp.concatenate(
        [
            jnp.sum(jnp.where(half, share, 0.0), axis=1, keepdims=True),
            jnp.sum(jnp.where(half, 0.0, share), axis=1, keepdims=True),
        ],
        axis=0,
    )
    n = [[sums[3 * i + j : 3 * i + j + 1] for j in range(3)] for i in range(4)]

    def form(p, q):
        value = 0.0
        for i, a in enumerate(p):
            line = 0.0
            for j, b in enumerate(q):
                line = line + n[i][j] * b
            value = value + a * line
        return value

    zero = jnp.zeros((1, 1), F32)
    one = jnp.ones((1, 1), F32)
    res_c = [one]
    dir_c = [one]
    sol_c = [zero, zero, zero]
    inner = form(res_c, res_c)
    for k in range(3):
        image_c = [zero] + dir_c
        image_c = [v + SHIFT * u for v, u in zip(image_c, dir_c + [zero])]
        step = inner / form(image_c, dir_c)
        for j, v in enumerate(dir_c):
            sol_c[j] = sol_c[j] + step * v
        res_c = [u - step * v for u, v in zip(res_c + [zero], image_c)]
        if k < 2:
            fresh = form(res_c, res_c)
            ratio = fresh / inner
            dir_c = [u + ratio * v for u, v in zip(res_c, dir_c + [zero])]
            inner = fresh
    answer = sum(sol_c[j] * preconds[j] for j in range(3))
    remain = sum(res_c[j] * residuals[j] for j in range(4))
    settle()
    out_ref[0] = answer
    out_ref[1] = remain


def on_device(slabs, subs, source, conductivity, basis, values, elements, owners, counts):
    rows = values.shape[0]
    zn = subs // XN
    kel = stencil_constants()
    vmem = pl.BlockSpec(memory_space=pltpu.VMEM)
    hbm = pl.BlockSpec(memory_space=pltpu.HBM)
    slot = zn * CAP
    peers = XN * (slabs // 2) - 1 + 1 + zn - 1
    dma = pltpu.SemaphoreType.DMA
    out = jax.ShapeDtypeStruct((2, EL, WIDE), F32)
    both = pl.pallas_call(
        functools.partial(kernel, slabs, subs),
        out_shape=out,
        in_specs=[hbm] * 8,
        out_specs=vmem,
        scratch_shapes=[
            pltpu.SMEM((EL,), F32),
            pltpu.SMEM((1,), jnp.int32),
            pltpu.VMEM((EL, NODES), F32),
            pltpu.VMEM((NB, EL, NODES), F32),
            pltpu.VMEM((NODES, rows), BF16),
            pltpu.VMEM((1, rows), jnp.int32),
            pltpu.VMEM((1, rows), jnp.int32),
            pltpu.VMEM((WIDE, WIDE), BF16),
            pltpu.VMEM((XN, slot, WIDE), BF16),
            pltpu.VMEM((XN, slot, WIDE), BF16),
            pltpu.VMEM((zn, EL, WIDE), F32),
            pltpu.VMEM((zn, EL, WIDE), F32),
            pltpu.VMEM((NB, EL * WIDE), F32),
            pltpu.VMEM((NB, EL * WIDE), F32),
            pltpu.VMEM((3, NB * EL, 128), F32),
            pltpu.VMEM((EL, WIDE), F32),
            pltpu.VMEM((2, 56, 128), F32),
            pltpu.VMEM((2, 56, 128), F32),
            pltpu.VMEM((3, 8, 128), F32),
            pltpu.VMEM((3, 4, 8, 128), F32),
            pltpu.VMEM((3, 8, 128), F32),
            pltpu.VMEM((peers, 8, 128), F32),
            dma((2, XN)),
            dma((2, zn)),
            dma((2, 2)),
            dma((2, 12)),
            dma((2, peers)),
            dma((8,)),
            pltpu.SemaphoreType.REGULAR,
        ],
        compiler_params=pltpu.CompilerParams(
            collective_id=0, has_side_effects=True, vmem_limit_bytes=60 * 1024 * 1024
        ),
    )(
        conductivity,
        counts,
        source,
        basis,
        values.T,
        elements.reshape(1, rows),
        owners.reshape(1, rows),
        jnp.asarray(kel, BF16),
    )
    return both[0, :, :NODES], both[1, :, :NODES]


def solution(mesh):
    both = ("slab", "sub")
    placed = (
        P(both, None),
        P(both),
        P(None, both, None),
        P(both, None),
        P(both),
        P(both, None),
        P(both),
    )
    return jax.shard_map(
        functools.partial(on_device, mesh.shape["slab"], mesh.shape["sub"]),
        mesh=mesh,
        in_specs=placed,
        out_specs=(P(both, None), P(both, None)),
        check_vma=False,
    )
```

```python
import functools

import jax
import jax.numpy as jnp
import numpy as np
from jax import lax
from jax.experimental import pallas as pl
from jax.experimental.pallas import tpu as pltpu
from jax.sharding import PartitionSpec as P

BLOCK = 128
CAP = 6
NODES = 343
WIDE = 384
FACE = 49
EL = 8
NB = 64
XN = 4
MARK = 120
EARLY = 24
SHIFT = 1.0
PENALTY = 10.0
RELAX = 0.2
HIGH = lax.Precision.HIGHEST
F32 = jnp.float32
BF16 = jnp.bfloat16
NT = (((1,), (1,)), ((), ()))
TN = (((0,), (0,)), ((), ()))


def stencil_constants():
    second = np.diag(np.array([1.0, 2, 2, 2, 2, 2, 1]))
    for i in range(6):
        second[i, i + 1] = second[i + 1, i] = -1.0
    one = np.eye(7)
    kel = (
        np.kron(np.kron(second, one), one)
        + np.kron(np.kron(one, second), one)
        + np.kron(one, np.kron(one, second))
    )
    full = np.zeros((WIDE, WIDE), np.float32)
    full[:NODES, :NODES] = kel
    full[NODES + 1] = np.diagonal(full)
    return full


def split2(value):
    hi = value.astype(BF16)
    lo = (value - hi.astype(F32)).astype(BF16)
    return hi, lo


def iota(shape, dim):
    return lax.broadcasted_iota(jnp.int32, shape, dim)


def dot(a, b, dims=(((1,), (0,)), ((), ())), precision=None):
    return lax.dot_general(a, b, dims, precision=precision, preferred_element_type=F32)


def kernel(
    slabs,
    subs,
    cond_ref,
    count_ref,
    src_ref,
    basis_ref,
    vals_ref,
    elem_ref,
    own_ref,
    kel_ref,
    out_ref,
    cond_in,
    count_in,
    src_in,
    basis_in,
    vals_in,
    elem_in,
    own_in,
    kel_in,
    a_src,
    a_dst,
    b_src,
    b_dst,
    bt_ref,
    cz_ref,
    padded,
    source_ref,
    g_src,
    g_dst,
    f_src,
    f_dst,
    s_src,
    s_dst,
    a_sem,
    b_sem,
    g_sem,
    f_sem,
    s_sem,
    in_sem,
    relay_sem,
):
    zn = subs // XN
    total = slabs * subs
    slab = lax.axis_index("slab")
    sub = lax.axis_index("sub")
    x = lax.rem(sub, XN)
    z = lax.div(sub, XN)
    chain = slab * subs + sub
    rows = vals_ref.shape[1]
    slot = zn * CAP

    def x_peer(i):
        return (slab, z * XN + lax.rem(x + i, XN))

    def z_peer(i):
        return (slab, lax.rem(z + i, zn) * XN + x)

    def plane_peer(i, j):
        return (lax.rem(slab + 2 * j, slabs), z * XN + lax.rem(x + i, XN))

    core_peer = (slab + 1 - 2 * lax.rem(slab, 2), sub)
    ys = slabs // 2
    far = sorted(range(1, zn), key=lambda i: -min(i, zn - i))
    plane = [(i, j) for i in range(XN) for j in range(ys) if i or j]
    plane.sort(key=lambda p: -min(p[0], XN - p[0]) - min(p[1], ys - p[1]))
    x_order = sorted(range(1, XN), key=lambda i: -min(i, XN - i))

    def chain_peer(step):
        other = lax.rem(chain + step + total, total)
        return (lax.div(other, subs), lax.rem(other, subs))

    reach = min(3, zn // 2)
    peers = (
        [z_peer(i) for i in far if min(i, zn - i) <= reach]
        + [(lax.rem(slab + i, slabs), sub) for i in range(1, slabs)]
        + [x_peer(i) for i in x_order]
    )
    barrier = pltpu.get_barrier_semaphore()
    for peer in peers:
        pl.semaphore_signal(
            barrier, inc=1, device_id=peer, device_id_type=pl.DeviceIdType.MESH
        )

    def send(src, dst, sems, k, peer):
        copy = pltpu.make_async_remote_copy(
            src_ref=src,
            dst_ref=dst,
            send_sem=sems.at[0, k],
            recv_sem=sems.at[1, k],
            device_id=peer,
            device_id_type=pl.DeviceIdType.MESH,
        )
        copy.start()
        return copy

    fetches = [
        pltpu.make_async_copy(src, dst, in_sem.at[k])
        for k, (src, dst) in enumerate(
            (
                (own_ref, own_in),
                (count_ref, count_in),
                (elem_ref, elem_in),
                (vals_ref, vals_in),
                (basis_ref, basis_in),
                (kel_ref, kel_in),
                (cond_ref, cond_in),
                (src_ref, src_in),
            )
        )
    ]
    for fetch in fetches:
        fetch.start()

    leaving = []

    def settle():
        while leaving:
            leaving.pop(0).wait_send()

    for fetch in fetches[:4]:
        fetch.wait()
    order = iota((subs, rows), 0)
    order = lax.rem(order, zn) * XN + lax.div(order, zn)
    live = lax.div(iota((subs, rows), 1), BLOCK) < count_in[0]
    owned = ((own_in[...] == order) & live).astype(F32)
    before = (iota((rows, rows), 0) < iota((rows, rows), 1)).astype(BF16)
    rank = dot(owned.astype(BF16), before)
    pieces = []
    for to in range(XN):
        mine = owned[to * zn : (to + 1) * zn]
        place = rank[to * zn : (to + 1) * zn]
        for j in range(CAP):
            pieces.append(jnp.where(place == float(j), mine, 0.0))
    select = jnp.concatenate(pieces, axis=0).astype(BF16)
    marks = (elem_in[...] == iota((128, rows), 0) - MARK).astype(BF16)
    moved = dot(select, vals_in[...], NT).astype(BF16)
    marked = dot(select, marks, NT).astype(BF16)
    a_src[:, :, :256] = moved[:, :256].reshape(XN, slot, 256)
    a_src[:, :, 256:] = marked.reshape(XN, slot, 128)
    a_src[:, :, 256:NODES] = moved[:, 256:].reshape(XN, slot, NODES - 256)

    pl.semaphore_wait(barrier, len(peers))
    hops = [h for h in (min(reach, zn // 2 - reach), zn // 2 - 2 * reach) if h > 0]

    def vouch(k):
        if k > 0 and k <= len(hops):
            pl.semaphore_wait(relay_sem.at[k - 1], 2)
        if k < len(hops):
            for peer in (z_peer(hops[k]), z_peer(zn - hops[k])):
                pl.semaphore_signal(
                    relay_sem.at[k],
                    inc=1,
                    device_id=peer,
                    device_id_type=pl.DeviceIdType.MESH,
                )

    a_copies = [
        send(a_src.at[lax.rem(x + i, XN)], a_dst.at[i], a_sem, i, x_peer(i))
        for i in x_order
    ]
    vouch(0)
    a_dst[0] = a_src[x]

    for fetch in fetches[4:]:
        fetch.wait()
    lane = iota((1, WIDE), 1)
    left = lane < FACE
    right = (lane >= NODES - FACE) & (lane < NODES)
    facew = jnp.where(left | right, PENALTY, 0.0)
    flat = basis_in[...].reshape(NB * EL, NODES)
    padded[2] = jnp.zeros((NB * EL, 128), F32)
    padded[0] = flat[:, 0:128]
    padded[1] = flat[:, 128:256]
    padded[2, :, : NODES - 256] = flat[:, 256:]
    for t in range(3):
        for e in range(EL):
            at = e * WIDE + t * 128
            bt_ref[:, at : at + 128] = padded[t, pl.ds(e, NB, stride=EL), :]

    def element(ref, e):
        return ref[:, e * WIDE : (e + 1) * WIDE]

    kel = kel_in[...]
    applied = []
    for e in range(EL):
        be = element(bt_ref, e)
        hi, lo = split2(be)
        stiff = dot(hi, kel) + dot(lo, kel)
        out = cond_in[e] * stiff + (RELAX + facew) * be
        if e > 0:
            turned = pltpu.roll(element(bt_ref, e - 1), WIDE - NODES + FACE, 1)
            out = out - jnp.where(left, PENALTY * turned, 0.0)
        if e < EL - 1:
            turned = pltpu.roll(element(bt_ref, e + 1), NODES - FACE, 1)
            out = out - jnp.where(right, PENALTY * turned, 0.0)
        applied.append(out)
    matrix = dot(bt_ref[...], jnp.concatenate(applied, axis=1), NT, HIGH)

    unit = (iota((NB, NB), 0) == iota((NB, NB), 1)).astype(F32)
    work = jnp.concatenate([matrix, unit], axis=1)
    row_id = iota((NB, 2 * NB), 0)

    def eliminate(work, k):
        row = work[k : k + 1, :] / work[k : k + 1, k : k + 1]
        return jnp.where(row_id == k, row, work - work[:, k : k + 1] * row)

    vouch(1)
    for k in range(EARLY):
        work = eliminate(work, k)

    for copy in a_copies:
        copy.wait_recv()
    arrived = a_dst[...].reshape(XN * slot, WIDE)
    pick = (iota((128, 128), 1) == MARK + lax.rem(iota((128, 128), 0), EL)).astype(BF16)
    spread = dot(pick, arrived[:, 256:], NT)
    keep = lax.rem(iota(spread.shape, 1), zn) == lax.div(iota(spread.shape, 0), EL)
    weights = jnp.where(keep, spread, 0.0).astype(BF16)
    sums = dot(weights, arrived)
    vouch(2)
    b_src[...] = sums[: zn * EL].reshape(zn, EL, WIDE)
    b_copies = [
        send(b_src.at[lax.rem(z + i, zn)], b_dst.at[i], b_sem, i, z_peer(i))
        for i in far
    ]
    b_dst[0] = b_src[z]
    leaving.extend(a_copies)
    settle()

    for k in range(EARLY, NB):
        work = eliminate(work, k)
    inverse = work[:, NB:]
    cz_ref[...] = dot(inverse, bt_ref[...], precision=HIGH)

    low = iota((1, 128), 1)
    near = low < FACE

    def left_face(value):
        return jnp.where(near, value[:, 0:128], 0.0)

    def right_face(value):
        return jnp.where(near, pltpu.roll(value[:, 256:WIDE], 128 - 38, 1), 0.0)

    w = PENALTY * (
        left_face(element(cz_ref, 0))
        + pltpu.roll(right_face(element(cz_ref, EL - 1)), 64, 1)
    )
    face_l = left_face(element(bt_ref, 0))
    face_r = right_face(element(bt_ref, EL - 1))
    g_src[0] = dot(face_l.T, w, precision=HIGH)[:56]
    g_src[1] = dot(face_r.T, w, precision=HIGH)[:56]
    el_row = iota((EL, WIDE), 0)
    conduct = jnp.zeros((EL, WIDE), F32)
    for e in range(EL):
        conduct = jnp.where(el_row == e, cond_in[e], conduct)
    kdiag = kel_in[NODES - 7 : NODES + 9].astype(F32)[8:9]
    diagonal = conduct * kdiag + RELAX + facew
    inner_lane = iota((EL, WIDE), 1) < NODES
    source_ref[:, 256:] = jnp.zeros((EL, 128), F32)
    source_ref[:, :NODES] = src_in[...]
    for copy in b_copies:
        copy.wait_recv()
    leaving.extend(b_copies)
    currents = b_dst[0]
    for i in range(1, zn):
        currents = currents + b_dst[i]
    rhs = source_ref[...] + jnp.where(inner_lane, currents, 0.0)

    has = {step: (chain + step >= 0) & (chain + step < total) for step in (-2, -1, 1, 2)}
    eye = iota((56, 128), 0) == iota((56, 128), 1)

    def turn(matrix, vector):
        column = jnp.sum(matrix * vector, axis=1, keepdims=True)
        return jnp.sum(jnp.where(eye, column, 0.0), axis=0, keepdims=True)

    def lift(column):
        line = jnp.sum(bt_ref[...] * column, axis=0, keepdims=True)
        return jnp.concatenate(
            [line[:, e * WIDE : (e + 1) * WIDE] for e in range(EL)], axis=0
        )

    def gram(a, b):
        prod = a * b
        prod = prod[:, 0:128] + prod[:, 128:256] + prod[:, 256:384]
        return jnp.sum(prod, axis=0, keepdims=True)

    pad_row = jnp.zeros((1, 256), F32)
    residuals, preconds = [rhs], []
    products = {}
    all_copies = []
    for k in range(3):
        res = residuals[k]
        scaled = res / diagonal
        acc = jnp.zeros((NB, WIDE), F32)
        for e in range(EL):
            acc = acc + element(cz_ref, e) * res[e : e + 1, :]
        acc = acc[:, 0:128] + acc[:, 128:256] + acc[:, 256:384]
        coarse = jnp.sum(acc, axis=1, keepdims=True)
        fl = jnp.sum(face_l * coarse, axis=0, keepdims=True)
        fr = jnp.sum(face_r * coarse, axis=0, keepdims=True)
        el = left_face(scaled[0:1]) + fl
        er = right_face(scaled[EL - 1 : EL]) + fr
        f_src[k] = jnp.concatenate([fl, fr, el, er, jnp.zeros((4, 128), F32)], axis=0)
        copies = [
            send(f_src.at[k], f_dst.at[k, i], f_sem, 4 * k + i, chain_peer(step))
            for i, step in ((2, -2), (3, 2), (0, -1), (1, 1))
        ]
        if k == 0:
            g_copies = [
                send(g_src.at[0], g_dst.at[0], g_sem, 0, chain_peer(-1)),
                send(g_src.at[1], g_dst.at[1], g_sem, 1, chain_peer(1)),
            ]
            leaving.extend(g_copies)
        settle()
        leaving.extend(copies)
        for i in range(k + 1):
            for j in range(k):
                if (i, j) not in products:
                    products[i, j] = gram(residuals[i], preconds[j])
        partial = scaled + lift(coarse)
        for copy in copies[2:]:
            copy.wait_recv()
        after1 = jnp.where(has[1], f_dst[k, 0], 0.0)
        before1 = jnp.where(has[-1], f_dst[k, 1], 0.0)
        own_v = before1[1:2] + pltpu.roll(after1[0:1], 64, 1)
        pre = partial + lift(jnp.sum(w * own_v, axis=1, keepdims=True))
        hi, lo = split2(pre)
        both = jnp.concatenate([hi.astype(F32), lo.astype(F32)], axis=0).astype(BF16)
        stiff = dot(both, kel)
        stiff = stiff[0:EL] + stiff[EL : 2 * EL]
        for copy in copies[:2] + (g_copies if k == 0 else []):
            copy.wait_recv()
        after2 = jnp.where(has[2], f_dst[k, 2], 0.0)
        before2 = jnp.where(has[-2], f_dst[k, 3], 0.0)
        after_v = fr + pltpu.roll(after2[0:1], 64, 1)
        before_v = before2[1:2] + pltpu.roll(fl, 64, 1)
        after_face = jnp.where(has[1], after1[2:3] + turn(g_dst[0], after_v), 0.0)
        before_face = jnp.where(has[-1], before1[3:4] + turn(g_dst[1], before_v), 0.0)
        from_left = pltpu.roll(pltpu.roll(pre, 1, 0), WIDE - NODES + FACE, 1)
        from_left = jnp.where(
            el_row == 0, jnp.concatenate([before_face, pad_row], axis=1), from_left
        )
        from_right = pltpu.roll(pltpu.roll(pre, EL - 1, 0), NODES - FACE, 1)
        from_right = jnp.where(
            el_row == EL - 1,
            jnp.concatenate([pad_row, pltpu.roll(after_face, 38, 1)], axis=1),
            from_right,
        )
        image = conduct * stiff + (RELAX + facew) * pre
        image = image - PENALTY * (
            jnp.where(left, from_left, 0.0) + jnp.where(right, from_right, 0.0)
        )
        preconds.append(pre)
        residuals.append(image - SHIFT * res)

    for i in range(4):
        for j in range(3):
            if (i, j) not in products:
                products[i, j] = gram(residuals[i], preconds[j])
    share = jnp.concatenate(
        [products[i, j] for i in range(4) for j in range(3)] + [jnp.zeros((4, 128), F32)], axis=0
    )
    half = iota((8, 128), 1) < 64
    share = share + pltpu.roll(share, 64, 1)
    share = jnp.where(half, share[0:8], share[8:16])
    at = 0
    stages = (
        [core_peer],
        [plane_peer(i, j) for i, j in plane],
        [z_peer(i) for i in far],
    )
    for stage, to in enumerate(stages):
        s_src[stage] = share
        copies = [
            send(s_src.at[stage], s_dst.at[at + i], s_sem, at + i, peer)
            for i, peer in enumerate(to)
        ]
        settle()
        leaving.extend(copies)
        for copy in copies:
            copy.wait_recv()
        for i in range(len(to)):
            share = share + s_dst[at + i]
        at += len(to)

    sums = jnp.concatenate(
        [
            jnp.sum(jnp.where(half, share, 0.0), axis=1, keepdims=True),
            jnp.sum(jnp.where(half, 0.0, share), axis=1, keepdims=True),
        ],
        axis=0,
    )
    n = [[sums[3 * i + j : 3 * i + j + 1] for j in range(3)] for i in range(4)]

    def form(p, q):
        value = 0.0
        for i, a in enumerate(p):
            line = 0.0
            for j, b in enumerate(q):
                line = line + n[i][j] * b
            value = value + a * line
        return value

    zero = jnp.zeros((1, 1), F32)
    one = jnp.ones((1, 1), F32)
    res_c = [one]
    dir_c = [one]
    sol_c = [zero, zero, zero]
    inner = form(res_c, res_c)
    for k in range(3):
        image_c = [zero] + dir_c
        image_c = [v + SHIFT * u for v, u in zip(image_c, dir_c + [zero])]
        step = inner / form(image_c, dir_c)
        for j, v in enumerate(dir_c):
            sol_c[j] = sol_c[j] + step * v
        res_c = [u - step * v for u, v in zip(res_c + [zero], image_c)]
        if k < 2:
            fresh = form(res_c, res_c)
            ratio = fresh / inner
            dir_c = [u + ratio * v for u, v in zip(res_c, dir_c + [zero])]
            inner = fresh
    answer = sum(sol_c[j] * preconds[j] for j in range(3))
    remain = sum(res_c[j] * residuals[j] for j in range(4))
    settle()
    out_ref[0] = answer
    out_ref[1] = remain


def on_device(slabs, subs, source, conductivity, basis, values, elements, owners, counts):
    rows = values.shape[0]
    zn = subs // XN
    kel = stencil_constants()
    vmem = pl.BlockSpec(memory_space=pltpu.VMEM)
    hbm = pl.BlockSpec(memory_space=pltpu.HBM)
    slot = zn * CAP
    peers = XN * (slabs // 2) - 1 + 1 + zn - 1
    dma = pltpu.SemaphoreType.DMA
    out = jax.ShapeDtypeStruct((2, EL, WIDE), F32)
    both = pl.pallas_call(
        functools.partial(kernel, slabs, subs),
        out_shape=out,
        in_specs=[hbm] * 8,
        out_specs=vmem,
        scratch_shapes=[
            pltpu.SMEM((EL,), F32),
            pltpu.SMEM((1,), jnp.int32),
            pltpu.VMEM((EL, NODES), F32),
            pltpu.VMEM((NB, EL, NODES), F32),
            pltpu.VMEM((NODES, rows), BF16),
            pltpu.VMEM((1, rows), jnp.int32),
            pltpu.VMEM((1, rows), jnp.int32),
            pltpu.VMEM((WIDE, WIDE), BF16),
            pltpu.VMEM((XN, slot, WIDE), BF16),
            pltpu.VMEM((XN, slot, WIDE), BF16),
            pltpu.VMEM((zn, EL, WIDE), F32),
            pltpu.VMEM((zn, EL, WIDE), F32),
            pltpu.VMEM((NB, EL * WIDE), F32),
            pltpu.VMEM((NB, EL * WIDE), F32),
            pltpu.VMEM((3, NB * EL, 128), F32),
            pltpu.VMEM((EL, WIDE), F32),
            pltpu.VMEM((2, 56, 128), F32),
            pltpu.VMEM((2, 56, 128), F32),
            pltpu.VMEM((3, 8, 128), F32),
            pltpu.VMEM((3, 4, 8, 128), F32),
            pltpu.VMEM((3, 8, 128), F32),
            pltpu.VMEM((peers, 8, 128), F32),
            dma((2, XN)),
            dma((2, zn)),
            dma((2, 2)),
            dma((2, 12)),
            dma((2, peers)),
            dma((8,)),
            pltpu.SemaphoreType.REGULAR((2,)),
        ],
        compiler_params=pltpu.CompilerParams(
            collective_id=0, has_side_effects=True, vmem_limit_bytes=60 * 1024 * 1024
        ),
    )(
        conductivity,
        counts,
        source,
        basis,
        values.T,
        elements.reshape(1, rows),
        owners.reshape(1, rows),
        jnp.asarray(kel, BF16),
    )
    return both[0, :, :NODES], both[1, :, :NODES]


def solution(mesh):
    both = ("slab", "sub")
    placed = (
        P(both, None),
        P(both),
        P(None, both, None),
        P(both, None),
        P(both),
        P(both, None),
        P(both),
    )
    return jax.shard_map(
        functools.partial(on_device, mesh.shape["slab"], mesh.shape["sub"]),
        mesh=mesh,
        in_specs=placed,
        out_specs=(P(both, None), P(both, None)),
        check_vma=False,
    )
```

```python
import functools

import jax
import jax.numpy as jnp
import numpy as np
from jax import lax
from jax.experimental import pallas as pl
from jax.experimental.pallas import tpu as pltpu
from jax.sharding import PartitionSpec as P

BLOCK = 128
CAP = 6
NODES = 343
WIDE = 384
FACE = 49
EL = 8
NB = 64
XN = 4
MARK = 120
EARLY = 24
SHIFT = 1.0
PENALTY = 10.0
RELAX = 0.2
HIGH = lax.Precision.HIGHEST
F32 = jnp.float32
BF16 = jnp.bfloat16
NT = (((1,), (1,)), ((), ()))
TN = (((0,), (0,)), ((), ()))


def stencil_constants():
    second = np.diag(np.array([1.0, 2, 2, 2, 2, 2, 1]))
    for i in range(6):
        second[i, i + 1] = second[i + 1, i] = -1.0
    one = np.eye(7)
    kel = (
        np.kron(np.kron(second, one), one)
        + np.kron(np.kron(one, second), one)
        + np.kron(one, np.kron(one, second))
    )
    full = np.zeros((WIDE, WIDE), np.float32)
    full[:NODES, :NODES] = kel
    full[NODES + 1] = np.diagonal(full)
    return full


def split2(value):
    hi = value.astype(BF16)
    lo = (value - hi.astype(F32)).astype(BF16)
    return hi, lo


def iota(shape, dim):
    return lax.broadcasted_iota(jnp.int32, shape, dim)


def dot(a, b, dims=(((1,), (0,)), ((), ())), precision=None):
    return lax.dot_general(a, b, dims, precision=precision, preferred_element_type=F32)


def kernel(
    slabs,
    subs,
    cond_ref,
    count_ref,
    src_ref,
    basis_ref,
    vals_ref,
    elem_ref,
    own_ref,
    kel_ref,
    out_ref,
    cond_in,
    count_in,
    src_in,
    basis_in,
    vals_in,
    elem_in,
    own_in,
    kel_in,
    a_src,
    a_dst,
    b_src,
    b_dst,
    bt_ref,
    cz_ref,
    padded,
    source_ref,
    g_src,
    g_dst,
    f_src,
    f_dst,
    s_src,
    s_dst,
    a_sem,
    b_sem,
    g_sem,
    f_sem,
    s_sem,
    in_sem,
    relay_sem,
):
    zn = subs // XN
    total = slabs * subs
    slab = lax.axis_index("slab")
    sub = lax.axis_index("sub")
    x = lax.rem(sub, XN)
    z = lax.div(sub, XN)
    chain = slab * subs + sub
    rows = vals_ref.shape[1]
    slot = zn * CAP

    def x_peer(i):
        return (slab, z * XN + lax.rem(x + i, XN))

    def z_peer(i):
        return (slab, lax.rem(z + i, zn) * XN + x)

    def plane_peer(i, j):
        return (lax.rem(slab + 2 * j, slabs), z * XN + lax.rem(x + i, XN))

    core_peer = (slab + 1 - 2 * lax.rem(slab, 2), sub)
    ys = slabs // 2
    far = sorted(range(1, zn), key=lambda i: -min(i, zn - i))
    plane = [(i, j) for i in range(XN) for j in range(ys) if i or j]
    plane.sort(key=lambda p: -min(p[0], XN - p[0]) - min(p[1], ys - p[1]))
    x_order = sorted(range(1, XN), key=lambda i: -min(i, XN - i))

    def chain_peer(step):
        other = lax.rem(chain + step + total, total)
        return (lax.div(other, subs), lax.rem(other, subs))

    reach = min(3, zn // 2)
    peers = (
        [z_peer(i) for i in far if min(i, zn - i) <= reach]
        + [(lax.rem(slab + i, slabs), sub) for i in range(1, slabs)]
        + [x_peer(i) for i in x_order]
    )
    barrier = pltpu.get_barrier_semaphore()
    for peer in peers:
        pl.semaphore_signal(
            barrier, inc=1, device_id=peer, device_id_type=pl.DeviceIdType.MESH
        )

    def send(src, dst, sems, k, peer):
        copy = pltpu.make_async_remote_copy(
            src_ref=src,
            dst_ref=dst,
            send_sem=sems.at[0, k],
            recv_sem=sems.at[1, k],
            device_id=peer,
            device_id_type=pl.DeviceIdType.MESH,
        )
        copy.start()
        return copy

    fetches = [
        pltpu.make_async_copy(src, dst, in_sem.at[k])
        for k, (src, dst) in enumerate(
            (
                (own_ref, own_in),
                (count_ref, count_in),
                (elem_ref, elem_in),
                (vals_ref, vals_in),
                (basis_ref, basis_in),
                (kel_ref, kel_in),
                (cond_ref, cond_in),
                (src_ref, src_in),
            )
        )
    ]
    for fetch in fetches:
        fetch.start()

    leaving = []

    def settle():
        while leaving:
            leaving.pop(0).wait_send()

    for fetch in fetches[:4]:
        fetch.wait()
    order = iota((subs, rows), 0)
    order = lax.rem(order, zn) * XN + lax.div(order, zn)
    live = lax.div(iota((subs, rows), 1), BLOCK) < count_in[0]
    owned = ((own_in[...] == order) & live).astype(F32)
    before = (iota((rows, rows), 0) < iota((rows, rows), 1)).astype(BF16)
    rank = dot(owned.astype(BF16), before)
    pieces = []
    for to in range(XN):
        mine = owned[to * zn : (to + 1) * zn]
        place = rank[to * zn : (to + 1) * zn]
        for j in range(CAP):
            pieces.append(jnp.where(place == float(j), mine, 0.0))
    select = jnp.concatenate(pieces, axis=0).astype(BF16)
    marks = (elem_in[...] == iota((128, rows), 0) - MARK).astype(BF16)
    moved = dot(select, vals_in[...], NT).astype(BF16)
    marked = dot(select, marks, NT).astype(BF16)
    a_src[:, :, :256] = moved[:, :256].reshape(XN, slot, 256)
    a_src[:, :, 256:] = marked.reshape(XN, slot, 128)
    a_src[:, :, 256:NODES] = moved[:, 256:].reshape(XN, slot, NODES - 256)

    pl.semaphore_wait(barrier, len(peers))
    hops = [h for h in (min(reach, zn // 2 - reach), zn // 2 - 2 * reach) if h > 0]

    def vouch(k):
        if k > 0 and k <= len(hops):
            pl.semaphore_wait(relay_sem.at[k - 1], 2)
        if k < len(hops):
            for peer in (z_peer(hops[k]), z_peer(zn - hops[k])):
                pl.semaphore_signal(
                    relay_sem.at[k],
                    inc=1,
                    device_id=peer,
                    device_id_type=pl.DeviceIdType.MESH,
                )

    parts = (slice(256, WIDE), slice(0, 256))
    a_parts = [
        [
            send(
                a_src.at[lax.rem(x + i, XN), :, part],
                a_dst.at[i, :, part],
                a_sem,
                p * XN + i,
                x_peer(i),
            )
            for i in x_order
        ]
        for p, part in enumerate(parts)
    ]
    vouch(0)
    a_dst[0] = a_src[x]

    for fetch in fetches[4:]:
        fetch.wait()
    lane = iota((1, WIDE), 1)
    left = lane < FACE
    right = (lane >= NODES - FACE) & (lane < NODES)
    facew = jnp.where(left | right, PENALTY, 0.0)
    flat = basis_in[...].reshape(NB * EL, NODES)
    padded[2] = jnp.zeros((NB * EL, 128), F32)
    padded[0] = flat[:, 0:128]
    padded[1] = flat[:, 128:256]
    padded[2, :, : NODES - 256] = flat[:, 256:]
    for t in range(3):
        for e in range(EL):
            at = e * WIDE + t * 128
            bt_ref[:, at : at + 128] = padded[t, pl.ds(e, NB, stride=EL), :]

    def element(ref, e):
        return ref[:, e * WIDE : (e + 1) * WIDE]

    kel = kel_in[...]
    applied = []
    for e in range(EL):
        be = element(bt_ref, e)
        hi, lo = split2(be)
        stiff = dot(hi, kel) + dot(lo, kel)
        out = cond_in[e] * stiff + (RELAX + facew) * be
        if e > 0:
            turned = pltpu.roll(element(bt_ref, e - 1), WIDE - NODES + FACE, 1)
            out = out - jnp.where(left, PENALTY * turned, 0.0)
        if e < EL - 1:
            turned = pltpu.roll(element(bt_ref, e + 1), NODES - FACE, 1)
            out = out - jnp.where(right, PENALTY * turned, 0.0)
        applied.append(out)
    matrix = dot(bt_ref[...], jnp.concatenate(applied, axis=1), NT, HIGH)

    unit = (iota((NB, NB), 0) == iota((NB, NB), 1)).astype(F32)
    work = jnp.concatenate([matrix, unit], axis=1)
    row_id = iota((NB, 2 * NB), 0)

    def eliminate(work, k):
        row = work[k : k + 1, :] / work[k : k + 1, k : k + 1]
        return jnp.where(row_id == k, row, work - work[:, k : k + 1] * row)

    vouch(1)
    for k in range(EARLY):
        work = eliminate(work, k)

    b_parts = []
    for p, part in enumerate(parts):
        for copy in a_parts[p]:
            copy.wait_recv()
        arrived = a_dst[:, :, part].reshape(XN * slot, part.stop - part.start)
        if p == 0:
            pick = iota((128, 128), 1) == MARK + lax.rem(iota((128, 128), 0), EL)
            spread = dot(pick.astype(BF16), arrived, NT)
            keep = lax.rem(iota(spread.shape, 1), zn) == lax.div(iota(spread.shape, 0), EL)
            weights = jnp.where(keep, spread, 0.0).astype(BF16)
        sums = dot(weights, arrived)[: zn * EL]
        b_src[:, :, part] = sums.reshape(zn, EL, part.stop - part.start)
        if p == 0:
            vouch(2)
        b_parts.append(
            [
                send(
                    b_src.at[lax.rem(z + i, zn), :, part],
                    b_dst.at[i, :, part],
                    b_sem,
                    p * zn + i,
                    z_peer(i),
                )
                for i in far
            ]
        )
    a_copies = a_parts[0] + a_parts[1]
    b_copies = b_parts[0] + b_parts[1]
    b_dst[0] = b_src[z]
    leaving.extend(a_copies)
    settle()

    for k in range(EARLY, NB):
        work = eliminate(work, k)
    inverse = work[:, NB:]
    cz_ref[...] = dot(inverse, bt_ref[...], precision=HIGH)

    low = iota((1, 128), 1)
    near = low < FACE

    def left_face(value):
        return jnp.where(near, value[:, 0:128], 0.0)

    def right_face(value):
        return jnp.where(near, pltpu.roll(value[:, 256:WIDE], 128 - 38, 1), 0.0)

    w = PENALTY * (
        left_face(element(cz_ref, 0))
        + pltpu.roll(right_face(element(cz_ref, EL - 1)), 64, 1)
    )
    face_l = left_face(element(bt_ref, 0))
    face_r = right_face(element(bt_ref, EL - 1))
    g_src[0] = dot(face_l.T, w, precision=HIGH)[:56]
    g_src[1] = dot(face_r.T, w, precision=HIGH)[:56]
    el_row = iota((EL, WIDE), 0)
    conduct = jnp.zeros((EL, WIDE), F32)
    for e in range(EL):
        conduct = jnp.where(el_row == e, cond_in[e], conduct)
    kdiag = kel_in[NODES - 7 : NODES + 9].astype(F32)[8:9]
    diagonal = conduct * kdiag + RELAX + facew
    inner_lane = iota((EL, WIDE), 1) < NODES
    source_ref[:, 256:] = jnp.zeros((EL, 128), F32)
    source_ref[:, :NODES] = src_in[...]
    for copy in b_copies:
        copy.wait_recv()
    leaving.extend(b_copies)
    currents = b_dst[0]
    for i in range(1, zn):
        currents = currents + b_dst[i]
    rhs = source_ref[...] + jnp.where(inner_lane, currents, 0.0)

    has = {step: (chain + step >= 0) & (chain + step < total) for step in (-2, -1, 1, 2)}
    eye = iota((56, 128), 0) == iota((56, 128), 1)

    def turn(matrix, vector):
        column = jnp.sum(matrix * vector, axis=1, keepdims=True)
        return jnp.sum(jnp.where(eye, column, 0.0), axis=0, keepdims=True)

    def lift(column):
        line = jnp.sum(bt_ref[...] * column, axis=0, keepdims=True)
        return jnp.concatenate(
            [line[:, e * WIDE : (e + 1) * WIDE] for e in range(EL)], axis=0
        )

    def gram(a, b):
        prod = a * b
        prod = prod[:, 0:128] + prod[:, 128:256] + prod[:, 256:384]
        return jnp.sum(prod, axis=0, keepdims=True)

    pad_row = jnp.zeros((1, 256), F32)
    residuals, preconds = [rhs], []
    products = {}
    all_copies = []
    for k in range(3):
        res = residuals[k]
        scaled = res / diagonal
        acc = jnp.zeros((NB, WIDE), F32)
        for e in range(EL):
            acc = acc + element(cz_ref, e) * res[e : e + 1, :]
        acc = acc[:, 0:128] + acc[:, 128:256] + acc[:, 256:384]
        coarse = jnp.sum(acc, axis=1, keepdims=True)
        fl = jnp.sum(face_l * coarse, axis=0, keepdims=True)
        fr = jnp.sum(face_r * coarse, axis=0, keepdims=True)
        el = left_face(scaled[0:1]) + fl
        er = right_face(scaled[EL - 1 : EL]) + fr
        f_src[k] = jnp.concatenate([fl, fr, el, er, jnp.zeros((4, 128), F32)], axis=0)
        copies = [
            send(f_src.at[k], f_dst.at[k, i], f_sem, 4 * k + i, chain_peer(step))
            for i, step in ((2, -2), (3, 2), (0, -1), (1, 1))
        ]
        if k == 0:
            g_copies = [
                send(g_src.at[0], g_dst.at[0], g_sem, 0, chain_peer(-1)),
                send(g_src.at[1], g_dst.at[1], g_sem, 1, chain_peer(1)),
            ]
            leaving.extend(g_copies)
        settle()
        leaving.extend(copies)
        for i in range(k + 1):
            for j in range(k):
                if (i, j) not in products:
                    products[i, j] = gram(residuals[i], preconds[j])
        partial = scaled + lift(coarse)
        for copy in copies[2:]:
            copy.wait_recv()
        after1 = jnp.where(has[1], f_dst[k, 0], 0.0)
        before1 = jnp.where(has[-1], f_dst[k, 1], 0.0)
        own_v = before1[1:2] + pltpu.roll(after1[0:1], 64, 1)
        pre = partial + lift(jnp.sum(w * own_v, axis=1, keepdims=True))
        hi, lo = split2(pre)
        both = jnp.concatenate([hi.astype(F32), lo.astype(F32)], axis=0).astype(BF16)
        stiff = dot(both, kel)
        stiff = stiff[0:EL] + stiff[EL : 2 * EL]
        for copy in copies[:2] + (g_copies if k == 0 else []):
            copy.wait_recv()
        after2 = jnp.where(has[2], f_dst[k, 2], 0.0)
        before2 = jnp.where(has[-2], f_dst[k, 3], 0.0)
        after_v = fr + pltpu.roll(after2[0:1], 64, 1)
        before_v = before2[1:2] + pltpu.roll(fl, 64, 1)
        after_face = jnp.where(has[1], after1[2:3] + turn(g_dst[0], after_v), 0.0)
        before_face = jnp.where(has[-1], before1[3:4] + turn(g_dst[1], before_v), 0.0)
        from_left = pltpu.roll(pltpu.roll(pre, 1, 0), WIDE - NODES + FACE, 1)
        from_left = jnp.where(
            el_row == 0, jnp.concatenate([before_face, pad_row], axis=1), from_left
        )
        from_right = pltpu.roll(pltpu.roll(pre, EL - 1, 0), NODES - FACE, 1)
        from_right = jnp.where(
            el_row == EL - 1,
            jnp.concatenate([pad_row, pltpu.roll(after_face, 38, 1)], axis=1),
            from_right,
        )
        image = conduct * stiff + (RELAX + facew) * pre
        image = image - PENALTY * (
            jnp.where(left, from_left, 0.0) + jnp.where(right, from_right, 0.0)
        )
        preconds.append(pre)
        residuals.append(image - SHIFT * res)

    for i in range(4):
        for j in range(3):
            if (i, j) not in products:
                products[i, j] = gram(residuals[i], preconds[j])
    share = jnp.concatenate(
        [products[i, j] for i in range(4) for j in range(3)] + [jnp.zeros((4, 128), F32)], axis=0
    )
    half = iota((8, 128), 1) < 64
    share = share + pltpu.roll(share, 64, 1)
    share = jnp.where(half, share[0:8], share[8:16])
    at = 0
    stages = (
        [core_peer],
        [plane_peer(i, j) for i, j in plane],
        [z_peer(i) for i in far],
    )
    for stage, to in enumerate(stages):
        s_src[stage] = share
        copies = [
            send(s_src.at[stage], s_dst.at[at + i], s_sem, at + i, peer)
            for i, peer in enumerate(to)
        ]
        settle()
        leaving.extend(copies)
        for copy in copies:
            copy.wait_recv()
        for i in range(len(to)):
            share = share + s_dst[at + i]
        at += len(to)

    sums = jnp.concatenate(
        [
            jnp.sum(jnp.where(half, share, 0.0), axis=1, keepdims=True),
            jnp.sum(jnp.where(half, 0.0, share), axis=1, keepdims=True),
        ],
        axis=0,
    )
    n = [[sums[3 * i + j : 3 * i + j + 1] for j in range(3)] for i in range(4)]

    def form(p, q):
        value = 0.0
        for i, a in enumerate(p):
            line = 0.0
            for j, b in enumerate(q):
                line = line + n[i][j] * b
            value = value + a * line
        return value

    zero = jnp.zeros((1, 1), F32)
    one = jnp.ones((1, 1), F32)
    res_c = [one]
    dir_c = [one]
    sol_c = [zero, zero, zero]
    inner = form(res_c, res_c)
    for k in range(3):
        image_c = [zero] + dir_c
        image_c = [v + SHIFT * u for v, u in zip(image_c, dir_c + [zero])]
        step = inner / form(image_c, dir_c)
        for j, v in enumerate(dir_c):
            sol_c[j] = sol_c[j] + step * v
        res_c = [u - step * v for u, v in zip(res_c + [zero], image_c)]
        if k < 2:
            fresh = form(res_c, res_c)
            ratio = fresh / inner
            dir_c = [u + ratio * v for u, v in zip(res_c, dir_c + [zero])]
            inner = fresh
    answer = sum(sol_c[j] * preconds[j] for j in range(3))
    remain = sum(res_c[j] * residuals[j] for j in range(4))
    settle()
    out_ref[0] = answer
    out_ref[1] = remain


def on_device(slabs, subs, source, conductivity, basis, values, elements, owners, counts):
    rows = values.shape[0]
    zn = subs // XN
    kel = stencil_constants()
    vmem = pl.BlockSpec(memory_space=pltpu.VMEM)
    hbm = pl.BlockSpec(memory_space=pltpu.HBM)
    slot = zn * CAP
    peers = XN * (slabs // 2) - 1 + 1 + zn - 1
    dma = pltpu.SemaphoreType.DMA
    out = jax.ShapeDtypeStruct((2, EL, WIDE), F32)
    both = pl.pallas_call(
        functools.partial(kernel, slabs, subs),
        out_shape=out,
        in_specs=[hbm] * 8,
        out_specs=vmem,
        scratch_shapes=[
            pltpu.SMEM((EL,), F32),
            pltpu.SMEM((1,), jnp.int32),
            pltpu.VMEM((EL, NODES), F32),
            pltpu.VMEM((NB, EL, NODES), F32),
            pltpu.VMEM((NODES, rows), BF16),
            pltpu.VMEM((1, rows), jnp.int32),
            pltpu.VMEM((1, rows), jnp.int32),
            pltpu.VMEM((WIDE, WIDE), BF16),
            pltpu.VMEM((XN, slot, WIDE), BF16),
            pltpu.VMEM((XN, slot, WIDE), BF16),
            pltpu.VMEM((zn, EL, WIDE), F32),
            pltpu.VMEM((zn, EL, WIDE), F32),
            pltpu.VMEM((NB, EL * WIDE), F32),
            pltpu.VMEM((NB, EL * WIDE), F32),
            pltpu.VMEM((3, NB * EL, 128), F32),
            pltpu.VMEM((EL, WIDE), F32),
            pltpu.VMEM((2, 56, 128), F32),
            pltpu.VMEM((2, 56, 128), F32),
            pltpu.VMEM((3, 8, 128), F32),
            pltpu.VMEM((3, 4, 8, 128), F32),
            pltpu.VMEM((3, 8, 128), F32),
            pltpu.VMEM((peers, 8, 128), F32),
            dma((2, 2 * XN)),
            dma((2, 2 * zn)),
            dma((2, 2)),
            dma((2, 12)),
            dma((2, peers)),
            dma((8,)),
            pltpu.SemaphoreType.REGULAR((2,)),
        ],
        compiler_params=pltpu.CompilerParams(
            collective_id=0, has_side_effects=True, vmem_limit_bytes=60 * 1024 * 1024
        ),
    )(
        conductivity,
        counts,
        source,
        basis,
        values.T,
        elements.reshape(1, rows),
        owners.reshape(1, rows),
        jnp.asarray(kel, BF16),
    )
    return both[0, :, :NODES], both[1, :, :NODES]


def solution(mesh):
    both = ("slab", "sub")
    placed = (
        P(both, None),
        P(both),
        P(None, both, None),
        P(both, None),
        P(both),
        P(both, None),
        P(both),
    )
    return jax.shard_map(
        functools.partial(on_device, mesh.shape["slab"], mesh.shape["sub"]),
        mesh=mesh,
        in_specs=placed,
        out_specs=(P(both, None), P(both, None)),
        check_vma=False,
    )
```

```python
import functools

import jax
import jax.numpy as jnp
import numpy as np
from jax import lax
from jax.experimental import pallas as pl
from jax.experimental.pallas import tpu as pltpu
from jax.sharding import PartitionSpec as P

BLOCK = 128
CAP = 6
NODES = 343
WIDE = 384
FACE = 49
EL = 8
NB = 64
XN = 4
MARK = 120
EARLY = 8
SHIFT = 1.0
PENALTY = 10.0
RELAX = 0.2
HIGH = lax.Precision.HIGHEST
F32 = jnp.float32
BF16 = jnp.bfloat16
NT = (((1,), (1,)), ((), ()))
TN = (((0,), (0,)), ((), ()))


def stencil_constants():
    second = np.diag(np.array([1.0, 2, 2, 2, 2, 2, 1]))
    for i in range(6):
        second[i, i + 1] = second[i + 1, i] = -1.0
    one = np.eye(7)
    kel = (
        np.kron(np.kron(second, one), one)
        + np.kron(np.kron(one, second), one)
        + np.kron(one, np.kron(one, second))
    )
    full = np.zeros((WIDE, WIDE), np.float32)
    full[:NODES, :NODES] = kel
    full[NODES + 1] = np.diagonal(full)
    return full


def split2(value):
    hi = value.astype(BF16)
    lo = (value - hi.astype(F32)).astype(BF16)
    return hi, lo


def iota(shape, dim):
    return lax.broadcasted_iota(jnp.int32, shape, dim)


def dot(a, b, dims=(((1,), (0,)), ((), ())), precision=None):
    return lax.dot_general(a, b, dims, precision=precision, preferred_element_type=F32)


def kernel(
    slabs,
    subs,
    cond_ref,
    count_ref,
    src_ref,
    basis_ref,
    vals_ref,
    elem_ref,
    own_ref,
    kel_ref,
    out_ref,
    cond_in,
    count_in,
    src_in,
    basis_in,
    vals_in,
    elem_in,
    own_in,
    kel_in,
    a_src,
    a_dst,
    b_src,
    b_dst,
    bt_ref,
    cz_ref,
    padded,
    source_ref,
    g_src,
    g_dst,
    f_src,
    f_dst,
    s_src,
    s_dst,
    a_sem,
    b_sem,
    g_sem,
    f_sem,
    s_sem,
    in_sem,
    relay_sem,
):
    zn = subs // XN
    total = slabs * subs
    slab = lax.axis_index("slab")
    sub = lax.axis_index("sub")
    x = lax.rem(sub, XN)
    z = lax.div(sub, XN)
    chain = slab * subs + sub
    rows = vals_ref.shape[1]
    slot = zn * CAP

    def x_peer(i):
        return (slab, z * XN + lax.rem(x + i, XN))

    def z_peer(i):
        return (slab, lax.rem(z + i, zn) * XN + x)

    def plane_peer(i, j):
        return (lax.rem(slab + 2 * j, slabs), z * XN + lax.rem(x + i, XN))

    core_peer = (slab + 1 - 2 * lax.rem(slab, 2), sub)
    ys = slabs // 2
    far = sorted(range(1, zn), key=lambda i: -min(i, zn - i))
    plane = [(i, j) for i in range(XN) for j in range(ys) if i or j]
    plane.sort(key=lambda p: -min(p[0], XN - p[0]) - min(p[1], ys - p[1]))
    x_order = sorted(range(1, XN), key=lambda i: -min(i, XN - i))

    def chain_peer(step):
        other = lax.rem(chain + step + total, total)
        return (lax.div(other, subs), lax.rem(other, subs))

    reach = min(3, zn // 2)
    peers = (
        [z_peer(i) for i in far if min(i, zn - i) <= reach]
        + [(lax.rem(slab + i, slabs), sub) for i in range(1, slabs)]
        + [x_peer(i) for i in x_order]
    )
    barrier = pltpu.get_barrier_semaphore()
    for peer in peers:
        pl.semaphore_signal(
            barrier, inc=1, device_id=peer, device_id_type=pl.DeviceIdType.MESH
        )

    def send(src, dst, sems, k, peer):
        copy = pltpu.make_async_remote_copy(
            src_ref=src,
            dst_ref=dst,
            send_sem=sems.at[0, k],
            recv_sem=sems.at[1, k],
            device_id=peer,
            device_id_type=pl.DeviceIdType.MESH,
        )
        copy.start()
        return copy

    fetches = [
        pltpu.make_async_copy(src, dst, in_sem.at[k])
        for k, (src, dst) in enumerate(
            (
                (own_ref, own_in),
                (count_ref, count_in),
                (elem_ref, elem_in),
                (vals_ref, vals_in),
                (basis_ref, basis_in),
                (kel_ref, kel_in),
                (cond_ref, cond_in),
                (src_ref, src_in),
            )
        )
    ]
    for fetch in fetches:
        fetch.start()

    leaving = []

    def settle():
        while leaving:
            leaving.pop(0).wait_send()

    for fetch in fetches[:4]:
        fetch.wait()
    order = iota((subs, rows), 0)
    order = lax.rem(order, zn) * XN + lax.div(order, zn)
    live = lax.div(iota((subs, rows), 1), BLOCK) < count_in[0]
    owned = ((own_in[...] == order) & live).astype(F32)
    before = (iota((rows, rows), 0) < iota((rows, rows), 1)).astype(BF16)
    rank = dot(owned.astype(BF16), before)
    pieces = []
    for to in range(XN):
        mine = owned[to * zn : (to + 1) * zn]
        place = rank[to * zn : (to + 1) * zn]
        for j in range(CAP):
            pieces.append(jnp.where(place == float(j), mine, 0.0))
    select = jnp.concatenate(pieces, axis=0).astype(BF16)
    marks = (elem_in[...] == iota((128, rows), 0) - MARK).astype(BF16)
    moved = dot(select, vals_in[...], NT).astype(BF16)
    marked = dot(select, marks, NT).astype(BF16)
    a_src[:, :, :256] = moved[:, :256].reshape(XN, slot, 256)
    a_src[:, :, 256:] = marked.reshape(XN, slot, 128)
    a_src[:, :, 256:NODES] = moved[:, 256:].reshape(XN, slot, NODES - 256)

    pl.semaphore_wait(barrier, len(peers))
    hops = [h for h in (min(reach, zn // 2 - reach), zn // 2 - 2 * reach) if h > 0]

    def vouch(k):
        if k > 0 and k <= len(hops):
            pl.semaphore_wait(relay_sem.at[k - 1], 2)
        if k < len(hops):
            for peer in (z_peer(hops[k]), z_peer(zn - hops[k])):
                pl.semaphore_signal(
                    relay_sem.at[k],
                    inc=1,
                    device_id=peer,
                    device_id_type=pl.DeviceIdType.MESH,
                )

    a_copies = [
        send(a_src.at[lax.rem(x + i, XN)], a_dst.at[i], a_sem, i, x_peer(i))
        for i in x_order
    ]
    vouch(0)
    a_dst[0] = a_src[x]

    for fetch in fetches[4:]:
        fetch.wait()
    lane = iota((1, WIDE), 1)
    left = lane < FACE
    right = (lane >= NODES - FACE) & (lane < NODES)
    facew = jnp.where(left | right, PENALTY, 0.0)
    flat = basis_in[...].reshape(NB * EL, NODES)
    padded[2] = jnp.zeros((NB * EL, 128), F32)
    padded[0] = flat[:, 0:128]
    padded[1] = flat[:, 128:256]
    padded[2, :, : NODES - 256] = flat[:, 256:]
    for t in range(3):
        for e in range(EL):
            at = e * WIDE + t * 128
            bt_ref[:, at : at + 128] = padded[t, pl.ds(e, NB, stride=EL), :]

    def element(ref, e):
        return ref[:, e * WIDE : (e + 1) * WIDE]

    kel = kel_in[...]
    applied = []
    for e in range(EL):
        be = element(bt_ref, e)
        hi, lo = split2(be)
        stiff = dot(hi, kel) + dot(lo, kel)
        out = cond_in[e] * stiff + (RELAX + facew) * be
        if e > 0:
            turned = pltpu.roll(element(bt_ref, e - 1), WIDE - NODES + FACE, 1)
            out = out - jnp.where(left, PENALTY * turned, 0.0)
        if e < EL - 1:
            turned = pltpu.roll(element(bt_ref, e + 1), NODES - FACE, 1)
            out = out - jnp.where(right, PENALTY * turned, 0.0)
        applied.append(out)
    matrix = dot(bt_ref[...], jnp.concatenate(applied, axis=1), NT, HIGH)

    unit = (iota((NB, NB), 0) == iota((NB, NB), 1)).astype(F32)
    work = jnp.concatenate([matrix, unit], axis=1)
    row_id = iota((NB, 2 * NB), 0)

    def eliminate(work, k):
        row = work[k : k + 1, :] / work[k : k + 1, k : k + 1]
        return jnp.where(row_id == k, row, work - work[:, k : k + 1] * row)

    vouch(1)
    for k in range(EARLY):
        work = eliminate(work, k)

    for copy in a_copies:
        copy.wait_recv()
    arrived = a_dst[...].reshape(XN * slot, WIDE)
    pick = (iota((128, 128), 1) == MARK + lax.rem(iota((128, 128), 0), EL)).astype(BF16)
    spread = dot(pick, arrived[:, 256:], NT)
    keep = lax.rem(iota(spread.shape, 1), zn) == lax.div(iota(spread.shape, 0), EL)
    weights = jnp.where(keep, spread, 0.0).astype(BF16)
    sums = dot(weights, arrived)
    vouch(2)
    b_src[...] = sums[: zn * EL].reshape(zn, EL, WIDE)
    b_copies = [
        send(b_src.at[lax.rem(z + i, zn)], b_dst.at[i], b_sem, i, z_peer(i))
        for i in far
    ]
    b_dst[0] = b_src[z]
    leaving.extend(a_copies)
    settle()

    for k in range(EARLY, NB):
        work = eliminate(work, k)
    inverse = work[:, NB:]
    cz_ref[...] = dot(inverse, bt_ref[...], precision=HIGH)

    low = iota((1, 128), 1)
    near = low < FACE

    def left_face(value):
        return jnp.where(near, value[:, 0:128], 0.0)

    def right_face(value):
        return jnp.where(near, pltpu.roll(value[:, 256:WIDE], 128 - 38, 1), 0.0)

    w = PENALTY * (
        left_face(element(cz_ref, 0))
        + pltpu.roll(right_face(element(cz_ref, EL - 1)), 64, 1)
    )
    face_l = left_face(element(bt_ref, 0))
    face_r = right_face(element(bt_ref, EL - 1))
    g_src[0] = dot(face_l.T, w, precision=HIGH)[:56]
    g_src[1] = dot(face_r.T, w, precision=HIGH)[:56]
    el_row = iota((EL, WIDE), 0)
    conduct = jnp.zeros((EL, WIDE), F32)
    for e in range(EL):
        conduct = jnp.where(el_row == e, cond_in[e], conduct)
    kdiag = kel_in[NODES - 7 : NODES + 9].astype(F32)[8:9]
    diagonal = conduct * kdiag + RELAX + facew
    inner_lane = iota((EL, WIDE), 1) < NODES
    source_ref[:, 256:] = jnp.zeros((EL, 128), F32)
    source_ref[:, :NODES] = src_in[...]
    for copy in b_copies:
        copy.wait_recv()
    leaving.extend(b_copies)
    currents = b_dst[0]
    for i in range(1, zn):
        currents = currents + b_dst[i]
    rhs = source_ref[...] + jnp.where(inner_lane, currents, 0.0)

    has = {step: (chain + step >= 0) & (chain + step < total) for step in (-2, -1, 1, 2)}
    eye = iota((56, 128), 0) == iota((56, 128), 1)

    def turn(matrix, vector):
        column = jnp.sum(matrix * vector, axis=1, keepdims=True)
        return jnp.sum(jnp.where(eye, column, 0.0), axis=0, keepdims=True)

    def lift(column):
        line = jnp.sum(bt_ref[...] * column, axis=0, keepdims=True)
        return jnp.concatenate(
            [line[:, e * WIDE : (e + 1) * WIDE] for e in range(EL)], axis=0
        )

    def gram(a, b):
        prod = a * b
        prod = prod[:, 0:128] + prod[:, 128:256] + prod[:, 256:384]
        return jnp.sum(prod, axis=0, keepdims=True)

    pad_row = jnp.zeros((1, 256), F32)
    residuals, preconds = [rhs], []
    products = {}
    all_copies = []
    for k in range(3):
        res = residuals[k]
        scaled = res / diagonal
        acc = jnp.zeros((NB, WIDE), F32)
        for e in range(EL):
            acc = acc + element(cz_ref, e) * res[e : e + 1, :]
        acc = acc[:, 0:128] + acc[:, 128:256] + acc[:, 256:384]
        coarse = jnp.sum(acc, axis=1, keepdims=True)
        fl = jnp.sum(face_l * coarse, axis=0, keepdims=True)
        fr = jnp.sum(face_r * coarse, axis=0, keepdims=True)
        el = left_face(scaled[0:1]) + fl
        er = right_face(scaled[EL - 1 : EL]) + fr
        f_src[k] = jnp.concatenate([fl, fr, el, er, jnp.zeros((4, 128), F32)], axis=0)
        copies = [
            send(f_src.at[k], f_dst.at[k, i], f_sem, 4 * k + i, chain_peer(step))
            for i, step in ((2, -2), (3, 2), (0, -1), (1, 1))
        ]
        if k == 0:
            g_copies = [
                send(g_src.at[0], g_dst.at[0], g_sem, 0, chain_peer(-1)),
                send(g_src.at[1], g_dst.at[1], g_sem, 1, chain_peer(1)),
            ]
            leaving.extend(g_copies)
        settle()
        leaving.extend(copies)
        for i in range(k + 1):
            for j in range(k):
                if (i, j) not in products:
                    products[i, j] = gram(residuals[i], preconds[j])
        partial = scaled + lift(coarse)
        for copy in copies[2:]:
            copy.wait_recv()
        after1 = jnp.where(has[1], f_dst[k, 0], 0.0)
        before1 = jnp.where(has[-1], f_dst[k, 1], 0.0)
        own_v = before1[1:2] + pltpu.roll(after1[0:1], 64, 1)
        pre = partial + lift(jnp.sum(w * own_v, axis=1, keepdims=True))
        hi, lo = split2(pre)
        both = jnp.concatenate([hi.astype(F32), lo.astype(F32)], axis=0).astype(BF16)
        stiff = dot(both, kel)
        stiff = stiff[0:EL] + stiff[EL : 2 * EL]
        for copy in copies[:2] + (g_copies if k == 0 else []):
            copy.wait_recv()
        after2 = jnp.where(has[2], f_dst[k, 2], 0.0)
        before2 = jnp.where(has[-2], f_dst[k, 3], 0.0)
        after_v = fr + pltpu.roll(after2[0:1], 64, 1)
        before_v = before2[1:2] + pltpu.roll(fl, 64, 1)
        after_face = jnp.where(has[1], after1[2:3] + turn(g_dst[0], after_v), 0.0)
        before_face = jnp.where(has[-1], before1[3:4] + turn(g_dst[1], before_v), 0.0)
        from_left = pltpu.roll(pltpu.roll(pre, 1, 0), WIDE - NODES + FACE, 1)
        from_left = jnp.where(
            el_row == 0, jnp.concatenate([before_face, pad_row], axis=1), from_left
        )
        from_right = pltpu.roll(pltpu.roll(pre, EL - 1, 0), NODES - FACE, 1)
        from_right = jnp.where(
            el_row == EL - 1,
            jnp.concatenate([pad_row, pltpu.roll(after_face, 38, 1)], axis=1),
            from_right,
        )
        image = conduct * stiff + (RELAX + facew) * pre
        image = image - PENALTY * (
            jnp.where(left, from_left, 0.0) + jnp.where(right, from_right, 0.0)
        )
        preconds.append(pre)
        residuals.append(image - SHIFT * res)

    for i in range(4):
        for j in range(3):
            if (i, j) not in products:
                products[i, j] = gram(residuals[i], preconds[j])
    share = jnp.concatenate(
        [products[i, j] for i in range(4) for j in range(3)] + [jnp.zeros((4, 128), F32)], axis=0
    )
    half = iota((8, 128), 1) < 64
    share = share + pltpu.roll(share, 64, 1)
    share = jnp.where(half, share[0:8], share[8:16])
    at = 0
    stages = (
        [core_peer],
        [plane_peer(i, j) for i, j in plane],
        [z_peer(i) for i in far],
    )
    for stage, to in enumerate(stages):
        s_src[stage] = share
        copies = [
            send(s_src.at[stage], s_dst.at[at + i], s_sem, at + i, peer)
            for i, peer in enumerate(to)
        ]
        settle()
        leaving.extend(copies)
        for copy in copies:
            copy.wait_recv()
        for i in range(len(to)):
            share = share + s_dst[at + i]
        at += len(to)

    sums = jnp.concatenate(
        [
            jnp.sum(jnp.where(half, share, 0.0), axis=1, keepdims=True),
            jnp.sum(jnp.where(half, 0.0, share), axis=1, keepdims=True),
        ],
        axis=0,
    )
    n = [[sums[3 * i + j : 3 * i + j + 1] for j in range(3)] for i in range(4)]

    def form(p, q):
        value = 0.0
        for i, a in enumerate(p):
            line = 0.0
            for j, b in enumerate(q):
                line = line + n[i][j] * b
            value = value + a * line
        return value

    zero = jnp.zeros((1, 1), F32)
    one = jnp.ones((1, 1), F32)
    res_c = [one]
    dir_c = [one]
    sol_c = [zero, zero, zero]
    inner = form(res_c, res_c)
    for k in range(3):
        image_c = [zero] + dir_c
        image_c = [v + SHIFT * u for v, u in zip(image_c, dir_c + [zero])]
        step = inner / form(image_c, dir_c)
        for j, v in enumerate(dir_c):
            sol_c[j] = sol_c[j] + step * v
        res_c = [u - step * v for u, v in zip(res_c + [zero], image_c)]
        if k < 2:
            fresh = form(res_c, res_c)
            ratio = fresh / inner
            dir_c = [u + ratio * v for u, v in zip(res_c, dir_c + [zero])]
            inner = fresh
    answer = sum(sol_c[j] * preconds[j] for j in range(3))
    remain = sum(res_c[j] * residuals[j] for j in range(4))
    settle()
    out_ref[0] = answer
    out_ref[1] = remain


def on_device(slabs, subs, source, conductivity, basis, values, elements, owners, counts):
    rows = values.shape[0]
    zn = subs // XN
    kel = stencil_constants()
    vmem = pl.BlockSpec(memory_space=pltpu.VMEM)
    hbm = pl.BlockSpec(memory_space=pltpu.HBM)
    slot = zn * CAP
    peers = XN * (slabs // 2) - 1 + 1 + zn - 1
    dma = pltpu.SemaphoreType.DMA
    out = jax.ShapeDtypeStruct((2, EL, WIDE), F32)
    both = pl.pallas_call(
        functools.partial(kernel, slabs, subs),
        out_shape=out,
        in_specs=[hbm] * 8,
        out_specs=vmem,
        scratch_shapes=[
            pltpu.SMEM((EL,), F32),
            pltpu.SMEM((1,), jnp.int32),
            pltpu.VMEM((EL, NODES), F32),
            pltpu.VMEM((NB, EL, NODES), F32),
            pltpu.VMEM((NODES, rows), BF16),
            pltpu.VMEM((1, rows), jnp.int32),
            pltpu.VMEM((1, rows), jnp.int32),
            pltpu.VMEM((WIDE, WIDE), BF16),
            pltpu.VMEM((XN, slot, WIDE), BF16),
            pltpu.VMEM((XN, slot, WIDE), BF16),
            pltpu.VMEM((zn, EL, WIDE), F32),
            pltpu.VMEM((zn, EL, WIDE), F32),
            pltpu.VMEM((NB, EL * WIDE), F32),
            pltpu.VMEM((NB, EL * WIDE), F32),
            pltpu.VMEM((3, NB * EL, 128), F32),
            pltpu.VMEM((EL, WIDE), F32),
            pltpu.VMEM((2, 56, 128), F32),
            pltpu.VMEM((2, 56, 128), F32),
            pltpu.VMEM((3, 8, 128), F32),
            pltpu.VMEM((3, 4, 8, 128), F32),
            pltpu.VMEM((3, 8, 128), F32),
            pltpu.VMEM((peers, 8, 128), F32),
            dma((2, XN)),
            dma((2, zn)),
            dma((2, 2)),
            dma((2, 12)),
            dma((2, peers)),
            dma((8,)),
            pltpu.SemaphoreType.REGULAR((2,)),
        ],
        compiler_params=pltpu.CompilerParams(
            collective_id=0, has_side_effects=True, vmem_limit_bytes=60 * 1024 * 1024
        ),
    )(
        conductivity,
        counts,
        source,
        basis,
        values.T,
        elements.reshape(1, rows),
        owners.reshape(1, rows),
        jnp.asarray(kel, BF16),
    )
    return both[0, :, :NODES], both[1, :, :NODES]


def solution(mesh):
    both = ("slab", "sub")
    placed = (
        P(both, None),
        P(both),
        P(None, both, None),
        P(both, None),
        P(both),
        P(both, None),
        P(both),
    )
    return jax.shard_map(
        functools.partial(on_device, mesh.shape["slab"], mesh.shape["sub"]),
        mesh=mesh,
        in_specs=placed,
        out_specs=(P(both, None), P(both, None)),
        check_vma=False,
    )
```
